128 devices in a mesh: tile: 16 (over x, z), section: 2 (over core), mode: 4 (over y).
Axes of the slice: x: 4, y: 4, z: 4, core: 2. Of those that a mesh axis runs over, the one named last changes fastest.
Arguments:
- object_slices: float32 [2, 8, 2048, 512], P(None, 'section', 'tile'), may hold values from -4 to 4
- probe_modes: float32 [2, 8, 128, 128], P(None, 'mode'), may hold values from -2.5 to 2.5
- propagator_phase: float32 [128, 128], replicated, may hold values from -3.140625 to 3.140625
- measured: float32 [64, 128, 128], P('tile'), may hold values from 0 to 2
- row_offset: int32 [64], P('tile'), may hold values from 0 to 127
- col_offset: int32 [64], P('tile'), may hold values from 0 to 384
- counts: int32 [16], P('tile'), may hold values from 1 to 4, 48 in all
Outputs:
- object_grad: float32 [2, 8, 2048, 512], P(None, 'section', 'tile', 'mode')
The draws below stay inside these ranges and needn't reach their ends.
Inputs may be any that keep to these rules, and one draw needn't show every extreme that they name: `counts`: the slots of a tile at or beyond its count are not part of the minibatch.
All inputs are finite; a program needn't handle non-finite values. No bound on the sum of `counts` on one device may be relied on, other than what follows from the above.
Results may differ from the reference program's by a relative error of at most 0.0003.
Values sent between devices are 32-bit elements; how exact they have to be, the bound alone decides.
A program may use at most 128 MiB of HBM per device.

```python
import math
import jax
import jax.numpy as jnp
import numpy as np
from jax import lax

W = 128
POS_MAX = 4
TILE_ROWS = 128
COLS = 512
MODES = 8
SLICES = 8
TILES = 16
POSITIONS = 64
ROWS = 2048
N_TILE = 16


def set_ends(values, key, smallest, top_value):
    extent = values.shape
    index_at = [jax.random.randint(jax.random.fold_in(key, axis), (), 0, extent[axis]) for axis in range(len(extent))]
    values = values.at[tuple(index_at)].set(smallest)
    longest = extent.index(max(extent))
    index_at[longest] = (index_at[longest] + 1) % extent[longest]
    return values.at[tuple(index_at)].set(top_value)


def block_scale(key, dims, split, smallest, largest):
    level, own = 1.0, jax.random.fold_in(key, 6)
    for position, blocks in split:
        heights = jnp.exp(jax.random.uniform(jax.random.fold_in(own, position), (blocks,), jnp.float32, smallest / len(split), largest / len(split)))
        level = level * jnp.repeat(heights, dims[position] // blocks).reshape([-1 if axis == position else 1 for axis in range(len(dims))])
    return level


def split_up(number_of, total, bound, skew):
    loads = [(1 << 20) // math.isqrt(standing ** skew) + 1 for standing in range(2, number_of + 1)]
    surplus, given = total - bound - (number_of - 1), [1] * (number_of - 1)
    while surplus > 0:
        free = [i for i in range(number_of - 1) if given[i] < bound]
        whole, budget = sum([loads[i] for i in free]), surplus
        for i in free:
            addition = min(bound - given[i], max(1, budget * loads[i] // whole), surplus)
            given[i] = given[i] + addition
            surplus = surplus - addition
    return np.array([bound] + given)


def uneven(stream_key, number_of, total, limit, lean):
    if number_of == 2:
        one = jax.random.randint(stream_key, (), max(1, total - limit), min(limit, total - 1) + 1)
        return jnp.stack([one, total - one])
    sizes = jnp.asarray(split_up(number_of, total, limit, lean), jnp.int32)
    couples = (number_of - 1) // 2
    source_of, receiver = sizes[1:1 + 2 * couples:2], sizes[2:2 + 2 * couples:2]
    margin = jnp.minimum(source_of - 1, limit - receiver)
    passed = jax.random.randint(jax.random.fold_in(stream_key, 1), (couples,), 0, 1 << 20) % (margin + 1)
    sizes = sizes.at[1:1 + 2 * couples:2].set(source_of - passed).at[2:2 + 2 * couples:2].set(receiver + passed)
    return sizes[jax.random.permutation(jax.random.fold_in(stream_key, 2), number_of)]


def scatter_about(stream_key, extent, width, bound, split=(), kind=jnp.bfloat16):
    gain = block_scale(stream_key, extent, split, -0.22, 0.18) if split else 1.0
    array = jax.random.normal(stream_key, extent, jnp.float32) * width * gain
    return jnp.minimum(jnp.maximum(array, -bound), bound).astype(kind)


def setup_inputs(seed: int = 0) -> dict:
    arg_keys = jax.random.split(jax.random.key(seed), 8)
    object_slices = scatter_about(arg_keys[0], (2, SLICES, ROWS, COLS), 0.72, 4.0, ((1, 2), (2, 16)), jnp.float32)
    probe_modes = scatter_about(arg_keys[1], (2, MODES, W, W), 0.25, 2.5, ((1, 4),), jnp.float32)
    propagator_phase = jnp.clip(jax.random.uniform(arg_keys[2], (W, W), jnp.float32, -3.140625, 3.140625), -3.140625, 3.140625)
    measured = jnp.clip(2.0 * jax.random.uniform(arg_keys[3], (POSITIONS, W, W), jnp.float32) ** block_scale(arg_keys[3], (POSITIONS, W, W), ((0, 16),), -0.2, 0.2), 0.0, 2.0)
    row_offset = set_ends(jax.random.randint(arg_keys[4], (POSITIONS,), 0, TILE_ROWS), jax.random.fold_in(arg_keys[4], 1), 0, TILE_ROWS - 1).astype(jnp.int32)
    col_offset = set_ends(jax.random.randint(arg_keys[5], (POSITIONS,), 0, COLS - W + 1), jax.random.fold_in(arg_keys[5], 1), 0, COLS - W).astype(jnp.int32)
    counts = uneven(arg_keys[6], TILES, 3 * N_TILE * POS_MAX // 4, POS_MAX, 2).astype(jnp.int32)
    return dict(object_slices=object_slices, probe_modes=probe_modes, propagator_phase=propagator_phase, measured=measured, row_offset=row_offset, col_offset=col_offset, counts=counts)


def reference(object_slices, probe_modes, propagator_phase, measured, row_offset, col_offset, counts):
    slot_index = jnp.arange(POSITIONS).astype(jnp.int32) % POS_MAX
    tile_index = jnp.arange(POSITIONS).astype(jnp.int32) // POS_MAX
    live_flag = (slot_index < counts[tile_index]).astype(object_slices.dtype)
    row_start = (tile_index * TILE_ROWS + row_offset).astype(jnp.int32)
    col_start = col_offset.astype(jnp.int32)
    kernel = lax.complex(jnp.cos(propagator_phase), jnp.sin(propagator_phase))
    first_wave = lax.complex(probe_modes[0], probe_modes[1])

    def total_loss(values):
        transmit = lax.complex(values[0], values[1])
        transmit = jnp.concatenate([transmit, transmit[:, :W]], axis=1)

        def single_loss(items):
            row_here, col_here, target, live_here = items
            window = lax.dynamic_slice(transmit, (jnp.int32(0), row_here, col_here), (SLICES, W, W))
            wavefield = first_wave
            for slice_index in range(SLICES):
                wavefield = wavefield * window[slice_index]
                wavefield = jnp.fft.ifft2(jnp.fft.fft2(wavefield, norm='ortho') * kernel, norm='ortho')
            farfield = jnp.fft.fft2(wavefield, norm='ortho')
            intensity = lax.optimization_barrier(jnp.sum(farfield.real ** 2 + farfield.imag ** 2, axis=0))
            return 0.5 * live_here * jnp.sum((intensity - target) ** 2)
        return jnp.sum(lax.map(single_loss, (row_start, col_start, measured, live_flag)))
    return jax.grad(total_loss)(object_slices)
```

```python
import functools
import math

import jax
import jax.numpy as jnp
import ml_dtypes
import numpy as np
from jax import lax
from jax.experimental import pallas as pl
from jax.experimental.pallas import tpu as pltpu
from jax.sharding import PartitionSpec as P

W = 128
SLICES = 8
LOCAL = 4
MODES = 4
SLOTS = 4
ROW_GROUP = 32
LAG_GATHER = 4
LAG_RIM = 8
MESH = pl.DeviceIdType.MESH


def tables():
    points = np.arange(W)
    angles = (points[:, None] * points[None, :] % W) * (-2.0 * math.pi / W)
    cos_table = np.cos(angles) / math.sqrt(W)
    sin_table = np.sin(angles) / math.sqrt(W)
    forward = np.block([[cos_table, sin_table], [-sin_table, cos_table]]).astype(np.float32)
    parts = []
    for table in (forward, forward.T):
        high = table.astype(ml_dtypes.bfloat16)
        parts += [high, (table - high.astype(np.float32)).astype(ml_dtypes.bfloat16)]
    return np.stack(parts)


def shifted(**steps):
    place = {}
    for axis, step in steps.items():
        size = lax.axis_size(axis)
        place[axis] = lax.rem(lax.axis_index(axis) + (step + size), size)
    return place


def dot(left, right):
    return jnp.dot(left, right, preferred_element_type=jnp.float32)


def stage(waves, high_table, low_table):
    out = []
    for wave in waves:
        high = wave.astype(jnp.bfloat16)
        low = (wave - high.astype(jnp.float32)).astype(jnp.bfloat16)
        out.append(dot(high, high_table) + dot(low, high_table) + dot(high, low_table))
    return out


def times(wave, real, imag):
    a, b = wave[:, :W], wave[:, W:]
    return jnp.concatenate([a * real - b * imag, a * imag + b * real], axis=1)


def times_conj(wave, real, imag):
    a, b = wave[:, :W], wave[:, W:]
    return jnp.concatenate([a * real + b * imag, b * real - a * imag], axis=1)


def turned(wave):
    return jnp.concatenate([wave[:, :W].T, wave[:, W:].T], axis=1)


def kernel(
    rows_ref, cols_ref, counts_ref, probe_ref, object_hbm, phase_hbm, measured_hbm, tables_hbm,
    out_ref,
    object_ref, phase_ref, measured_ref, tables_ref,
    cols_send, cols_recv, probes, halo_send, halo_recv, windows, saved, turn, far, current,
    power_send, power_recv, terms, terms_recv, sums, groups, rim_send, rim_recv, own_part,
    load_sem, cols_sem, probe_send_sem, probe_recv_sem, halo_send_sem, halo_recv_sem,
    window_send_sem, window_recv_sem, power_sem, terms_send_sem, terms_recv_sem,
    group_send_sem, group_recv_sem, rim_send_sem, rim_recv_sem, out_send_sem, out_recv_sem,
):
    section = lax.axis_index("section")
    me = lax.axis_index("mode")
    peer = shifted(section=1)

    loads = [
        pltpu.make_async_copy(object_hbm, object_ref, load_sem.at[0]),
        pltpu.make_async_copy(phase_hbm, phase_ref, load_sem.at[1]),
        pltpu.make_async_copy(measured_hbm.at[me], measured_ref, load_sem.at[2]),
        pltpu.make_async_copy(tables_hbm, tables_ref, load_sem.at[3]),
    ]
    for load in loads:
        load.start()

    barrier = pltpu.get_barrier_semaphore()
    partners = [peer, shifted(mode=1), shifted(mode=2), shifted(mode=3), shifted(tile=1), shifted(tile=-1)]
    for partner in partners:
        pl.semaphore_signal(barrier, 1, device_id=partner, device_id_type=MESH)
    pl.semaphore_wait(barrier, len(partners))

    def remote(source, target, send_sem, recv_sem, device):
        return pltpu.make_async_remote_copy(
            src_ref=source, dst_ref=target, send_sem=send_sem, recv_sem=recv_sem,
            device_id=device, device_id_type=MESH,
        )

    def behind(distance):
        return lax.rem(me + (SLOTS - distance), SLOTS)

    def ahead(distance):
        return lax.rem(me + distance, SLOTS)

    def group_rows(index):
        return pl.ds(pl.multiple_of(index * ROW_GROUP, ROW_GROUP), ROW_GROUP)

    cols_copy = remote(cols_send, cols_recv, cols_sem.at[0], cols_sem.at[1], shifted(tile=1))

    def probe_copy(distance):
        return remote(
            probe_ref.at[:, section], probes.at[distance],
            probe_send_sem.at[distance], probe_recv_sem.at[distance], shifted(mode=distance),
        )

    def halo_copy(local):
        return remote(
            halo_send.at[local], halo_recv.at[local],
            halo_send_sem.at[local], halo_recv_sem.at[local], shifted(tile=-1),
        )

    def window_copy(index):
        return remote(
            windows.at[index], windows.at[index],
            window_send_sem.at[index], window_recv_sem.at[index], peer,
        )

    power_copy = remote(power_send, power_recv, power_sem.at[0], power_sem.at[1], peer)

    def terms_copy(index):
        local = lax.rem(index, LOCAL)
        return remote(
            terms.at[index], terms_recv.at[local],
            terms_send_sem.at[local], terms_recv_sem.at[local], peer,
        )

    def group_copy(local, distance):
        return remote(
            sums.at[local, :, group_rows(ahead(distance))], groups.at[local, distance],
            group_send_sem.at[local, distance], group_recv_sem.at[local, distance],
            shifted(mode=distance),
        )

    def rim_copy(local):
        return remote(
            rim_send.at[local], rim_recv.at[local],
            rim_send_sem.at[local], rim_recv_sem.at[local], shifted(tile=1),
        )

    def out_copy(local, distance, place):
        return remote(
            own_part.at[local, ahead(distance)], out_ref.at[:, local, group_rows(place)],
            out_send_sem.at[local, distance], out_recv_sem.at[local, distance],
            shifted(mode=distance),
        )

    first_row, first_col = rows_ref[me], cols_ref[me]

    cols_send[...] = jnp.full((8, W), first_col, jnp.int32)
    cols_copy.start()
    for distance in (1, 3, 2):
        probe_copy(distance).start()

    lane = lax.broadcasted_iota(jnp.int32, (8, W), 1)
    row_index = lax.broadcasted_iota(jnp.int32, (W, W), 0)

    def chosen(component, local, block):
        value = object_ref[component, local, :, 0:W]
        for index in range(1, 4):
            value = jnp.where(block == index, object_ref[component, local, :, index * W:(index + 1) * W], value)
        return value

    def block_of(cols):
        return jnp.broadcast_to(((cols + (W - 1) - lane) // W)[0:1], (W, W))

    def send_halo(local):
        block = block_of(cols_recv[...])
        for component in range(2):
            halo_send[local, component] = chosen(component, local, block)
        halo_copy(local).start()

    for load in loads[1:]:
        load.wait()
    phase = phase_ref[...].T
    turn[0] = jnp.cos(phase)
    turn[1] = jnp.sin(phase)
    power_recv_turned = measured_ref[...].T
    measured_ref[...] = power_recv_turned
    for component in range(2):
        probes[0, component] = probe_ref[component, section]
    loads[0].wait()
    cols_copy.wait()

    @pl.when(section == 0)
    def _():
        def each(local, carry):
            send_halo(local)
            return carry

        lax.fori_loop(0, LOCAL, each, 0)

    for distance in (1, 3, 2):
        probe_copy(distance).wait()

    def place_probe(mode, carry):
        for component in range(2):
            value = pltpu.roll(probes[mode, component], first_row, 0)
            value = pltpu.roll(value, lax.rem(first_col, W), 1)
            current[mode, :, component * W:(component + 1) * W] = value
        return carry

    lax.fori_loop(0, MODES, place_probe, 0)

    def prepare(index):
        local = lax.rem(index, LOCAL)
        owner = index // LOCAL == section

        @pl.when(owner)
        def _():
            halo_copy(local).wait_recv()
            block = block_of(jnp.full((8, W), first_col, jnp.int32))
            for component in range(2):
                windows[index, component] = jnp.where(
                    row_index >= first_row, chosen(component, local, block), halo_recv[local, component]
                )
            window_copy(index).start()

        @pl.when(jnp.logical_not(owner))
        def _():
            window_copy(index).wait_recv()

        for step, locals_sent in ((0, (0, 1)), (2, (2, 3))):
            @pl.when((section == 1) & (index == step))
            def _():
                for local_sent in locals_sent:
                    send_halo(local_sent)

    forward = (tables_ref.at[0], tables_ref.at[1])
    inverse = (tables_ref.at[2], tables_ref.at[3])

    def run(waves, which):
        return stage(waves, which[0][...], which[1][...])

    def entered(index):
        real, imag = windows[index, 0], windows[index, 1]
        waves = []
        for mode in range(MODES):
            wave = current[mode]
            saved[index, mode] = wave
            waves.append(times(wave, real, imag))
        return waves

    def forward_step(index, carry):
        prepare(index)
        waves = [turned(wave) for wave in run(entered(index), forward)]
        waves = [times(wave, turn[0], turn[1]) for wave in run(waves, forward)]
        waves = [turned(wave) for wave in run(waves, inverse)]
        waves = run(waves, inverse)
        for mode in range(MODES):
            current[mode] = waves[mode]
        return carry

    lax.fori_loop(0, SLICES - 1, forward_step, 0)
    prepare(SLICES - 1)
    waves = [turned(wave) for wave in run(entered(SLICES - 1), forward)]
    waves = [times(wave, turn[0], turn[1]) for wave in run(waves, forward)]
    power = jnp.zeros((W, W), jnp.float32)
    for mode in range(MODES):
        far[mode] = waves[mode]
        power += waves[mode][:, :W] * waves[mode][:, :W] + waves[mode][:, W:] * waves[mode][:, W:]
    power_send[...] = power
    power_copy.start()
    power_copy.wait()
    live = jnp.where(me < counts_ref[0], 2.0, 0.0).astype(jnp.float32)
    residual = live * (power_send[...] + power_recv[...] - measured_ref[...])
    residual = jnp.concatenate([residual, residual], axis=1)
    waves = [times_conj(residual * far[mode], turn[0], turn[1]) for mode in range(MODES)]
    waves = [turned(wave) for wave in run(waves, inverse)]
    waves = run(waves, inverse)
    for mode in range(MODES):
        current[mode] = waves[mode]

    def gather_terms(index):
        local = lax.rem(index, LOCAL)
        terms_copy(index).wait_recv()
        for component in range(2):
            sums[local, component] = terms[index, component] + terms_recv[local, component]
        for distance in (2, 1, 3):
            group_copy(local, distance).start()

    def sort_groups(index):
        local = lax.rem(index, LOCAL)
        for distance in (1, 3, 2):
            group_copy(local, distance).wait_recv()
        for component in range(2):
            groups[local, 0, component] = sums[local, component, group_rows(me)]
        rows_here = me * ROW_GROUP + lax.broadcasted_iota(jnp.int32, (ROW_GROUP, W), 0)
        lanes_here = lax.broadcasted_iota(jnp.int32, (ROW_GROUP, W), 1)
        keys = []
        for distance in range(SLOTS):
            slot = behind(distance)
            block = (cols_ref[slot] + (W - 1) - lanes_here) // W
            keys.append(jnp.where(rows_here >= rows_ref[slot], block, block + SLOTS))
        for component in range(2):
            values = [groups[local, distance, component] for distance in range(SLOTS)]
            for target in range(2 * SLOTS):
                total = jnp.zeros((ROW_GROUP, W), jnp.float32)
                for distance in range(SLOTS):
                    total += jnp.where(keys[distance] == target, values[distance], 0.0)
                if target < SLOTS:
                    own_part[local, target, component] = total
                else:
                    rim_send[local, target - SLOTS, component] = total
        rim_copy(local).start()

    def finish(index):
        local = lax.rem(index, LOCAL)
        rim_copy(local).wait_recv()
        for target in range(SLOTS):
            for component in range(2):
                own_part[local, target, component] += rim_recv[local, target, component]
        for distance in (2, 1, 3):
            out_copy(local, distance, me).start()
        for component in range(2):
            out_ref[component, local, group_rows(me)] = own_part[local, me, component]

    def backward_step(step, carry):
        index = SLICES - 1 - step

        @pl.when(step < SLICES)
        def _():
            total_real = jnp.zeros((W, W), jnp.float32)
            total_imag = jnp.zeros((W, W), jnp.float32)
            for mode in range(MODES):
                wave, start = current[mode], saved[index, mode]
                a, b = wave[:, :W], wave[:, W:]
                c, d = start[:, :W], start[:, W:]
                total_real += c * a + d * b
                total_imag += c * b - d * a
            terms[index, 0] = total_real
            terms[index, 1] = total_imag

            @pl.when(index // LOCAL != section)
            def _():
                terms_copy(index).start()

        @pl.when(step < SLICES - 1)
        def _():
            real, imag = windows[index, 0], windows[index, 1]
            waves = [times_conj(current[mode], real, imag) for mode in range(MODES)]
            waves = [turned(wave) for wave in run(waves, forward)]
            waves = [times_conj(wave, turn[0], turn[1]) for wave in run(waves, forward)]
            waves = [turned(wave) for wave in run(waves, inverse)]
            waves = run(waves, inverse)
            for mode in range(MODES):
                current[mode] = waves[mode]

        for lag, action in ((1, gather_terms), (LAG_GATHER, sort_groups), (LAG_RIM, finish)):
            late = index + lag

            @pl.when((late >= 0) & (late < SLICES) & (late // LOCAL == section))
            def _():
                action(late)

        return carry

    lax.fori_loop(0, SLICES + LAG_RIM, backward_step, 0)

    for distance in (1, 3, 2):
        for local in range(LOCAL):
            out_copy(local, distance, behind(distance)).wait_recv()

    def drain(local, carry):
        halo_copy(local).wait_send()
        window_copy(section * LOCAL + local).wait_send()
        terms_copy((1 - section) * LOCAL + local).wait_send()
        rim_copy(local).wait_send()
        for distance in (1, 2, 3):
            group_copy(local, distance).wait_send()
            out_copy(local, distance, me).wait_send()
        return carry

    lax.fori_loop(0, LOCAL, drain, 0)


def body(object_slices, probe_modes, propagator_phase, measured, row_offset, col_offset, counts):
    square = (W, W)
    vmem = lambda *shape: pltpu.VMEM(shape, jnp.float32)
    dma = lambda *shape: pltpu.SemaphoreType.DMA(shape)
    smem_spec = pl.BlockSpec(memory_space=pltpu.SMEM)
    vmem_spec = pl.BlockSpec(memory_space=pltpu.VMEM)
    any_spec = pl.BlockSpec(memory_space=pl.ANY)
    return pl.pallas_call(
        kernel,
        out_shape=jax.ShapeDtypeStruct((2, LOCAL) + square, jnp.float32),
        in_specs=[smem_spec] * 3 + [vmem_spec] + [any_spec] * 4,
        out_specs=vmem_spec,
        scratch_shapes=[
            vmem(*object_slices.shape), vmem(*square), vmem(*square),
            pltpu.VMEM((4, 2 * W, 2 * W), jnp.bfloat16),
            pltpu.VMEM((8, W), jnp.int32), pltpu.VMEM((8, W), jnp.int32),
            vmem(MODES, 2, *square),
            vmem(LOCAL, 2, *square), vmem(LOCAL, 2, *square),
            vmem(SLICES, 2, *square),
            vmem(SLICES, MODES, W, 2 * W),
            vmem(2, *square),
            vmem(MODES, W, 2 * W), vmem(MODES, W, 2 * W),
            vmem(*square), vmem(*square),
            vmem(SLICES, 2, *square), vmem(LOCAL, 2, *square),
            vmem(LOCAL, 2, *square),
            vmem(LOCAL, SLOTS, 2, ROW_GROUP, W),
            vmem(LOCAL, SLOTS, 2, ROW_GROUP, W), vmem(LOCAL, SLOTS, 2, ROW_GROUP, W),
            vmem(LOCAL, SLOTS, 2, ROW_GROUP, W),
            dma(4), dma(2), dma(4), dma(4), dma(LOCAL), dma(LOCAL),
            dma(SLICES), dma(SLICES), dma(2), dma(LOCAL), dma(LOCAL),
            dma(LOCAL, SLOTS), dma(LOCAL, SLOTS), dma(LOCAL), dma(LOCAL),
            dma(LOCAL, SLOTS), dma(LOCAL, SLOTS),
        ],
        compiler_params=pltpu.CompilerParams(
            collective_id=0, has_side_effects=True, vmem_limit_bytes=40 * 1024 * 1024
        ),
    )(row_offset, col_offset, counts, probe_modes, object_slices, propagator_phase, measured, jnp.asarray(tables()))


def solution(mesh):
    in_specs = (
        P(None, "section", "tile", None),
        P(None, "mode", None, None),
        P(),
        P("tile", None, None),
        P("tile"),
        P("tile"),
        P("tile"),
    )
    out_specs = P(None, "section", "tile", "mode")
    return jax.shard_map(body, mesh=mesh, in_specs=in_specs, out_specs=out_specs, check_vma=False)
```

```python
import functools
import math

import jax
import jax.numpy as jnp
import ml_dtypes
import numpy as np
from jax import lax
from jax.experimental import pallas as pl
from jax.experimental.pallas import tpu as pltpu
from jax.sharding import PartitionSpec as P

W = 128
SLICES = 8
LOCAL = 4
MODES = 4
SLOTS = 4
EARLY = 1
ROW_GROUP = 32
LAG_GATHER = 4
LAG_RIM = 8
MESH = pl.DeviceIdType.MESH


def tables():
    points = np.arange(W)
    angles = (points[:, None] * points[None, :] % W) * (-2.0 * math.pi / W)
    cos_table = np.cos(angles) / math.sqrt(W)
    sin_table = np.sin(angles) / math.sqrt(W)
    forward = np.block([[cos_table, sin_table], [-sin_table, cos_table]]).astype(np.float32)
    parts = []
    for table in (forward, forward.T):
        high = table.astype(ml_dtypes.bfloat16)
        parts += [high, (table - high.astype(np.float32)).astype(ml_dtypes.bfloat16)]
    return np.stack(parts)


def shifted(**steps):
    place = {}
    for axis, step in steps.items():
        size = lax.axis_size(axis)
        place[axis] = lax.rem(lax.axis_index(axis) + (step + size), size)
    return place


def dot(left, right):
    return jnp.dot(left, right, preferred_element_type=jnp.float32)


def stage(waves, high_table, low_table):
    out = []
    for wave in waves:
        high = wave.astype(jnp.bfloat16)
        low = (wave - high.astype(jnp.float32)).astype(jnp.bfloat16)
        out.append(dot(high, high_table) + dot(low, high_table) + dot(high, low_table))
    return out


def times(wave, real, imag):
    a, b = wave[:, :W], wave[:, W:]
    return jnp.concatenate([a * real - b * imag, a * imag + b * real], axis=1)


def times_conj(wave, real, imag):
    a, b = wave[:, :W], wave[:, W:]
    return jnp.concatenate([a * real + b * imag, b * real - a * imag], axis=1)


def turned(wave):
    return jnp.concatenate([wave[:, :W].T, wave[:, W:].T], axis=1)


def kernel(
    rows_hbm, cols_hbm, counts_ref, probe_hbm, object_hbm, phase_hbm, measured_hbm, tables_hbm,
    out_ref,
    rows_ref, cols_ref, object_ref, phase_ref, measured_ref, tables_ref,
    info_send, info_recv, info_ref, keys_ref, probes, halo_send, halo_recv, windows, saved, turn, far, current,
    power_send, power_recv, terms, terms_recv, sums, groups, rim_send, rim_recv, own_part,
    small_sem, load_sem, info_sem, measured_sem, probe_send_sem, probe_recv_sem, halo_send_sem, halo_recv_sem,
    window_send_sem, window_recv_sem, power_sem, terms_send_sem, terms_recv_sem,
    group_send_sem, group_recv_sem, rim_send_sem, rim_recv_sem, out_send_sem, out_recv_sem,
):
    section = lax.axis_index("section")
    me = lax.axis_index("mode")
    peer = shifted(section=1)

    loads = [
        pltpu.make_async_copy(object_hbm, object_ref, load_sem.at[0]),
        pltpu.make_async_copy(phase_hbm, phase_ref, load_sem.at[1]),
        pltpu.make_async_copy(tables_hbm, tables_ref, load_sem.at[2]),
        pltpu.make_async_copy(probe_hbm.at[:, section], probes.at[0], load_sem.at[3]),
    ]
    small_loads = [
        pltpu.make_async_copy(source, target, small_sem.at[index])
        for index, (source, target) in enumerate(
            ((rows_hbm, rows_ref), (cols_hbm, cols_ref))
        )
    ]
    for load in small_loads + loads:
        load.start()

    barrier = pltpu.get_barrier_semaphore()
    partners = [peer, shifted(mode=1), shifted(mode=2), shifted(mode=3), shifted(tile=1), shifted(tile=-1)]
    for partner in partners:
        pl.semaphore_signal(barrier, 1, device_id=partner, device_id_type=MESH)

    def remote(source, target, send_sem, recv_sem, device):
        return pltpu.make_async_remote_copy(
            src_ref=source, dst_ref=target, send_sem=send_sem, recv_sem=recv_sem,
            device_id=device, device_id_type=MESH,
        )

    def behind(distance):
        return lax.rem(me + (SLOTS - distance), SLOTS)

    def ahead(distance):
        return lax.rem(me + distance, SLOTS)

    def group_rows(index):
        return pl.ds(pl.multiple_of(index * ROW_GROUP, ROW_GROUP), ROW_GROUP)

    info_copy = remote(info_send, info_recv, info_sem.at[0], info_sem.at[1], shifted(tile=1))
    measured_copy = remote(
        measured_hbm.at[me], measured_ref, measured_sem.at[0], measured_sem.at[1], shifted(tile=1)
    )

    def probe_copy(distance):
        return remote(
            probe_hbm.at[:, section], probes.at[distance],
            probe_send_sem.at[distance], probe_recv_sem.at[distance], shifted(mode=distance),
        )

    def halo_copy(local):
        return remote(
            halo_send.at[local], halo_recv.at[local],
            halo_send_sem.at[local], halo_recv_sem.at[local], shifted(tile=1),
        )

    def window_copy(index):
        return remote(
            windows.at[index], windows.at[index],
            window_send_sem.at[index], window_recv_sem.at[index], peer,
        )

    power_copy = remote(power_send, power_recv, power_sem.at[0], power_sem.at[1], peer)

    def terms_copy(index):
        local = lax.rem(index, LOCAL)
        return remote(
            terms.at[index], terms_recv.at[local],
            terms_send_sem.at[local], terms_recv_sem.at[local], peer,
        )

    def group_copy(local, distance):
        return remote(
            sums.at[local, :, group_rows(ahead(distance))], groups.at[local, distance],
            group_send_sem.at[local, distance], group_recv_sem.at[local, distance],
            shifted(mode=distance),
        )

    def rim_copy(local):
        return remote(
            rim_send.at[local], rim_recv.at[local],
            rim_send_sem.at[local], rim_recv_sem.at[local], shifted(tile=-1),
        )

    def out_copy(local, distance, place):
        return remote(
            own_part.at[local, ahead(distance)], out_ref.at[:, local, group_rows(place)],
            out_send_sem.at[local, distance], out_recv_sem.at[local, distance],
            shifted(mode=distance),
        )

    lane = lax.broadcasted_iota(jnp.int32, (8, W), 1)
    row_index = lax.broadcasted_iota(jnp.int32, (W, W), 0)

    def chosen(component, local, block):
        value = object_ref[component, local, :, 0:W]
        for index in range(1, 4):
            value = jnp.where(block == index, object_ref[component, local, :, index * W:(index + 1) * W], value)
        return value

    def block_of(first):
        return jnp.broadcast_to(((jnp.full((8, W), first, jnp.int32) + (W - 1) - lane) // W)[0:1], (W, W))

    for load in small_loads:
        load.wait()
    for slot in range(SLOTS):
        info_send[slot] = jnp.full((8, W), rows_ref[slot], jnp.int32)
        info_send[SLOTS + slot] = jnp.full((8, W), cols_ref[slot], jnp.int32)
    info_send[2 * SLOTS] = jnp.full((8, W), counts_ref[0], jnp.int32)
    loads[0].wait()
    sent_block = block_of(cols_ref[me])

    def cut(local, carry):
        for component in range(2):
            halo_send[local, component] = chosen(component, local, sent_block)
        return carry

    lax.fori_loop(0, LOCAL, cut, 0)
    for load in loads[1:]:
        load.wait()
    phase = phase_ref[...].T
    turn[0] = jnp.cos(phase)
    turn[1] = jnp.sin(phase)

    pl.semaphore_wait(barrier, len(partners))
    info_copy.start()

    @pl.when(section == 0)
    def _():
        halo_copy(0).start()

    for distance in (1, 3, 2):
        probe_copy(distance).start()

    @pl.when(section == 0)
    def _():
        for local in range(1, LOCAL):
            halo_copy(local).start()

    measured_copy.start()
    info_copy.wait()
    info_load = pltpu.make_async_copy(info_recv, info_ref, load_sem.at[4])
    info_load.start()
    info_load.wait()

    def row_of(slot):
        return info_ref[slot, 0, 0]

    def col_of(slot):
        return info_ref[SLOTS + slot, 0, 0]

    first_row, first_col = row_of(me), col_of(me)

    rows_here = me * ROW_GROUP + lax.broadcasted_iota(jnp.int32, (ROW_GROUP, W), 0)
    lanes_here = lax.broadcasted_iota(jnp.int32, (ROW_GROUP, W), 1)
    for distance in range(SLOTS):
        slot = behind(distance)
        block = (col_of(slot) + (W - 1) - lanes_here) // W
        keys_ref[distance] = jnp.where(rows_here >= row_of(slot), block + SLOTS, block)

    def place_probe(mode):
        for component in range(2):
            value = pltpu.roll(probes[mode, component], first_row, 0)
            value = pltpu.roll(value, lax.rem(first_col, W), 1)
            current[mode, :, component * W:(component + 1) * W] = value

    place_probe(0)
    for distance in (1, 3):
        probe_copy(distance).wait()
        place_probe(distance)

    def prepare(index):
        local = lax.rem(index, LOCAL)
        owner = index // LOCAL == section

        @pl.when(owner)
        def _():
            halo_copy(local).wait_recv()
            block = block_of(first_col)
            for component in range(2):
                windows[index, component] = jnp.where(
                    row_index >= first_row, halo_recv[local, component], chosen(component, local, block)
                )
            window_copy(index).start()

        @pl.when(jnp.logical_not(owner))
        def _():
            window_copy(index).wait_recv()

        for step, locals_sent in ((0, (0, 1)), (2, (2, 3))):
            @pl.when((section == 1) & (index == step))
            def _():
                for local_sent in locals_sent:
                    halo_copy(local_sent).start()

    forward = (tables_ref.at[0], tables_ref.at[1])
    inverse = (tables_ref.at[2], tables_ref.at[3])

    def run(waves, which):
        return stage(waves, which[0][...], which[1][...])

    def entered(index, modes):
        real, imag = windows[index, 0], windows[index, 1]
        waves = []
        for mode in modes:
            wave = current[mode]
            saved[index, mode] = wave
            waves.append(times(wave, real, imag))
        return waves

    def advance(index, modes):
        waves = [turned(wave) for wave in run(entered(index, modes), forward)]
        waves = [times(wave, turn[0], turn[1]) for wave in run(waves, forward)]
        waves = [turned(wave) for wave in run(waves, inverse)]
        waves = run(waves, inverse)
        for mode, wave in zip(modes, waves):
            current[mode] = wave

    everything = tuple(range(MODES))

    def early_step(index, carry):
        prepare(index)
        advance(index, (0, 1, 3))
        return carry

    lax.fori_loop(0, EARLY, early_step, 0)
    probe_copy(2).wait()
    place_probe(2)
    for index in range(EARLY):
        advance(index, (2,))

    def forward_pair(step, carry):
        index = EARLY + 2 * step
        prepare(index)
        prepare(index + 1)
        advance(index, everything)
        advance(index + 1, everything)
        return carry

    pairs = (SLICES - 1 - EARLY) // 2
    lax.fori_loop(0, pairs, forward_pair, 0)
    for index in range(EARLY + 2 * pairs, SLICES - 1):
        prepare(index)
        advance(index, everything)
    prepare(SLICES - 1)
    waves = [turned(wave) for wave in run(entered(SLICES - 1, everything), forward)]
    waves = [times(wave, turn[0], turn[1]) for wave in run(waves, forward)]
    power = jnp.zeros((W, W), jnp.float32)
    for mode in range(MODES):
        far[mode] = waves[mode]
        power += waves[mode][:, :W] * waves[mode][:, :W] + waves[mode][:, W:] * waves[mode][:, W:]
    power_send[...] = power
    power_copy.start()
    measured_copy.wait()
    power_copy.wait()
    live = jnp.where(me < info_ref[2 * SLOTS, 0, 0], 2.0, 0.0).astype(jnp.float32)
    residual = live * (power_send[...] + power_recv[...] - measured_ref[...].T)
    residual = jnp.concatenate([residual, residual], axis=1)
    waves = [times_conj(residual * far[mode], turn[0], turn[1]) for mode in range(MODES)]
    waves = [turned(wave) for wave in run(waves, inverse)]
    waves = run(waves, inverse)
    for mode in range(MODES):
        current[mode] = waves[mode]

    def gather_terms(index):
        local = lax.rem(index, LOCAL)
        terms_copy(index).wait_recv()
        for component in range(2):
            sums[local, component] = terms[index, component] + terms_recv[local, component]
        for distance in (2, 1, 3):
            group_copy(local, distance).start()

    def sort_groups(index):
        local = lax.rem(index, LOCAL)
        for distance in (1, 3, 2):
            group_copy(local, distance).wait_recv()
        for component in range(2):
            groups[local, 0, component] = sums[local, component, group_rows(me)]
        keys = [keys_ref[distance] for distance in range(SLOTS)]
        for component in range(2):
            values = [groups[local, distance, component] for distance in range(SLOTS)]
            for target in range(2 * SLOTS):
                total = jnp.zeros((ROW_GROUP, W), jnp.float32)
                for distance in range(SLOTS):
                    total += jnp.where(keys[distance] == target, values[distance], 0.0)
                if target < SLOTS:
                    own_part[local, target, component] = total
                else:
                    rim_send[local, target - SLOTS, component] = total
        rim_copy(local).start()

    def finish(index):
        local = lax.rem(index, LOCAL)
        rim_copy(local).wait_recv()
        for target in range(SLOTS):
            for component in range(2):
                own_part[local, target, component] += rim_recv[local, target, component]
        for distance in (2, 1, 3):
            out_copy(local, distance, me).start()
        for component in range(2):
            out_ref[component, local, group_rows(me)] = own_part[local, me, component]

    def collect(index):
        total_real = jnp.zeros((W, W), jnp.float32)
        total_imag = jnp.zeros((W, W), jnp.float32)
        for mode in range(MODES):
            wave, start = current[mode], saved[index, mode]
            a, b = wave[:, :W], wave[:, W:]
            c, d = start[:, :W], start[:, W:]
            total_real += c * a + d * b
            total_imag += c * b - d * a
        terms[index, 0] = total_real
        terms[index, 1] = total_imag

    def hand_over(index):
        @pl.when(index // LOCAL != section)
        def _():
            terms_copy(index).start()

    def retreat(index):
        real, imag = windows[index, 0], windows[index, 1]
        waves = [times_conj(current[mode], real, imag) for mode in range(MODES)]
        waves = [turned(wave) for wave in run(waves, forward)]
        waves = [times_conj(wave, turn[0], turn[1]) for wave in run(waves, forward)]
        waves = [turned(wave) for wave in run(waves, inverse)]
        waves = run(waves, inverse)
        for mode in range(MODES):
            current[mode] = waves[mode]

    def deliver(index, lags):
        for lag, action in lags:
            late = index + lag

            @pl.when((late >= 0) & (late < SLICES) & (late // LOCAL == section))
            def _():
                action(late)

    lags = ((1, gather_terms), (LAG_GATHER, sort_groups), (LAG_RIM, finish))

    def backward_pair(step, carry):
        index = SLICES - 1 - 2 * step
        collect(index)
        hand_over(index)
        retreat(index)
        collect(index - 1)
        retreat(index - 1)
        hand_over(index - 1)
        deliver(index, lags)
        deliver(index - 1, lags)
        return carry

    lax.fori_loop(0, SLICES // 2 - 1, backward_pair, 0)
    collect(1)
    hand_over(1)
    retreat(1)
    deliver(1, lags)
    collect(0)
    hand_over(0)

    def drain_step(step, carry):
        deliver(-step, lags)
        return carry

    lax.fori_loop(0, LAG_RIM + 1, drain_step, 0)

    for distance in (1, 3, 2):
        for local in range(LOCAL):
            out_copy(local, distance, behind(distance)).wait_recv()

    def drain(local, carry):
        halo_copy(local).wait_send()
        window_copy(section * LOCAL + local).wait_send()
        terms_copy((1 - section) * LOCAL + local).wait_send()
        rim_copy(local).wait_send()
        for distance in (1, 2, 3):
            group_copy(local, distance).wait_send()
            out_copy(local, distance, me).wait_send()
        return carry

    lax.fori_loop(0, LOCAL, drain, 0)


def body(object_slices, probe_modes, propagator_phase, measured, row_offset, col_offset, counts):
    square = (W, W)
    vmem = lambda *shape: pltpu.VMEM(shape, jnp.float32)
    dma = lambda *shape: pltpu.SemaphoreType.DMA(shape)
    smem_spec = pl.BlockSpec(memory_space=pltpu.SMEM)
    vmem_spec = pl.BlockSpec(memory_space=pltpu.VMEM)
    hbm_spec = pl.BlockSpec(memory_space=pltpu.HBM)
    operands = (
        row_offset, col_offset, counts, probe_modes, object_slices, propagator_phase, measured,
        jnp.asarray(tables()),
    )
    operands = [
        operand if operand is counts else pltpu.with_memory_space_constraint(operand, pltpu.HBM)
        for operand in operands
    ]
    return pl.pallas_call(
        kernel,
        out_shape=jax.ShapeDtypeStruct((2, LOCAL) + square, jnp.float32),
        in_specs=[hbm_spec] * 2 + [smem_spec] + [hbm_spec] * 5,
        out_specs=vmem_spec,
        scratch_shapes=[
            pltpu.SMEM((SLOTS,), jnp.int32), pltpu.SMEM((SLOTS,), jnp.int32),
            vmem(*object_slices.shape), vmem(*square), vmem(*square),
            pltpu.VMEM((4, 2 * W, 2 * W), jnp.bfloat16),
            pltpu.VMEM((2 * SLOTS + 1, 8, W), jnp.int32), pltpu.VMEM((2 * SLOTS + 1, 8, W), jnp.int32),
            pltpu.SMEM((2 * SLOTS + 1, 8, W), jnp.int32),
            pltpu.VMEM((SLOTS, ROW_GROUP, W), jnp.int32),
            vmem(MODES, 2, *square),
            vmem(LOCAL, 2, *square), vmem(LOCAL, 2, *square),
            vmem(SLICES, 2, *square),
            vmem(SLICES, MODES, W, 2 * W),
            vmem(2, *square),
            vmem(MODES, W, 2 * W), vmem(MODES, W, 2 * W),
            vmem(*square), vmem(*square),
            vmem(SLICES, 2, *square), vmem(LOCAL, 2, *square),
            vmem(LOCAL, 2, *square),
            vmem(LOCAL, SLOTS, 2, ROW_GROUP, W),
            vmem(LOCAL, SLOTS, 2, ROW_GROUP, W), vmem(LOCAL, SLOTS, 2, ROW_GROUP, W),
            vmem(LOCAL, SLOTS, 2, ROW_GROUP, W),
            dma(2), dma(5), dma(2), dma(2), dma(4), dma(4), dma(LOCAL), dma(LOCAL),
            dma(SLICES), dma(SLICES), dma(2), dma(LOCAL), dma(LOCAL),
            dma(LOCAL, SLOTS), dma(LOCAL, SLOTS), dma(LOCAL), dma(LOCAL),
            dma(LOCAL, SLOTS), dma(LOCAL, SLOTS),
        ],
        compiler_params=pltpu.CompilerParams(
            collective_id=0, has_side_effects=True, vmem_limit_bytes=40 * 1024 * 1024
        ),
    )(*operands)


def solution(mesh):
    in_specs = (
        P(None, "section", "tile", None),
        P(None, "mode", None, None),
        P(),
        P("tile", None, None),
        P("tile"),
        P("tile"),
        P("tile"),
    )
    out_specs = P(None, "section", "tile", "mode")
    return jax.shard_map(body, mesh=mesh, in_specs=in_specs, out_specs=out_specs, check_vma=False)
```

```python
import functools
import math

import jax
import jax.numpy as jnp
import ml_dtypes
import numpy as np
from jax import lax
from jax.experimental import pallas as pl
from jax.experimental.pallas import tpu as pltpu
from jax.sharding import PartitionSpec as P

W = 128
SLICES = 8
LOCAL = 4
MODES = 4
SLOTS = 4
EARLY = 0
ROW_GROUP = 32
LAG_TERMS = 0
LAG_GATHER = 3
LAG_RIM = 7
MESH = pl.DeviceIdType.MESH


def tables():
    points = np.arange(W)
    angles = (points[:, None] * points[None, :] % W) * (-2.0 * math.pi / W)
    cos_table = np.cos(angles) / math.sqrt(W)
    sin_table = np.sin(angles) / math.sqrt(W)
    forward = np.block([[cos_table, sin_table], [-sin_table, cos_table]]).astype(np.float32)
    parts = []
    for table in (forward, forward.T):
        high = table.astype(ml_dtypes.bfloat16)
        parts += [high, (table - high.astype(np.float32)).astype(ml_dtypes.bfloat16)]
    return np.stack(parts)


def shifted(**steps):
    place = {}
    for axis, step in steps.items():
        size = lax.axis_size(axis)
        place[axis] = lax.rem(lax.axis_index(axis) + (step + size), size)
    return place


def dot(left, right):
    return jnp.dot(left, right, preferred_element_type=jnp.float32)


def stage(waves, high_table, low_table):
    out = []
    for wave in waves:
        high = wave.astype(jnp.bfloat16)
        low = (wave - high.astype(jnp.float32)).astype(jnp.bfloat16)
        out.append(dot(high, high_table) + dot(low, high_table) + dot(high, low_table))
    return out


def times(wave, real, imag):
    a, b = wave[:, :W], wave[:, W:]
    return jnp.concatenate([a * real - b * imag, a * imag + b * real], axis=1)


def times_conj(wave, real, imag):
    a, b = wave[:, :W], wave[:, W:]
    return jnp.concatenate([a * real + b * imag, b * real - a * imag], axis=1)


def turned(wave):
    return jnp.concatenate([wave[:, :W].T, wave[:, W:].T], axis=1)


def kernel(
    rows_hbm, cols_hbm, counts_ref, probe_hbm, object_hbm, phase_hbm, measured_hbm, tables_hbm,
    out_ref,
    rows_ref, cols_ref, object_ref, phase_ref, measured_ref, tables_ref,
    info_send, info_recv, info_ref, keys_ref, probes, halo_send, halo_recv, windows, saved, turn, far, current,
    power_send, power_recv, terms, terms_recv, sums, groups, rim_send, rim_recv, own_part,
    small_sem, load_sem, info_sem, measured_sem, probe_send_sem, probe_recv_sem, halo_send_sem, halo_recv_sem,
    window_send_sem, window_recv_sem, power_sem, terms_send_sem, terms_recv_sem,
    group_send_sem, group_recv_sem, rim_send_sem, rim_recv_sem, out_send_sem, out_recv_sem,
):
    section = lax.axis_index("section")
    me = lax.axis_index("mode")
    peer = shifted(section=1)

    loads = [
        pltpu.make_async_copy(object_hbm, object_ref, load_sem.at[0]),
        pltpu.make_async_copy(phase_hbm, phase_ref, load_sem.at[1]),
        pltpu.make_async_copy(tables_hbm, tables_ref, load_sem.at[2]),
        pltpu.make_async_copy(probe_hbm.at[:, section], probes.at[0], load_sem.at[3]),
    ]
    small_loads = [
        pltpu.make_async_copy(source, target, small_sem.at[index])
        for index, (source, target) in enumerate(
            ((rows_hbm, rows_ref), (cols_hbm, cols_ref))
        )
    ]
    for load in small_loads + loads:
        load.start()

    barrier = pltpu.get_barrier_semaphore()
    partners = [peer, shifted(mode=1), shifted(mode=2), shifted(mode=3), shifted(tile=1), shifted(tile=-1)]
    for partner in partners:
        pl.semaphore_signal(barrier, 1, device_id=partner, device_id_type=MESH)

    def remote(source, target, send_sem, recv_sem, device):
        return pltpu.make_async_remote_copy(
            src_ref=source, dst_ref=target, send_sem=send_sem, recv_sem=recv_sem,
            device_id=device, device_id_type=MESH,
        )

    def behind(distance):
        return lax.rem(me + (SLOTS - distance), SLOTS)

    def ahead(distance):
        return lax.rem(me + distance, SLOTS)

    def group_rows(index):
        return pl.ds(pl.multiple_of(index * ROW_GROUP, ROW_GROUP), ROW_GROUP)

    info_copy = remote(info_send, info_recv, info_sem.at[0], info_sem.at[1], shifted(tile=1))
    measured_copy = remote(
        measured_hbm.at[me], measured_ref, measured_sem.at[0], measured_sem.at[1], shifted(tile=1)
    )

    def probe_copy(distance):
        return remote(
            probe_hbm.at[:, section], probes.at[distance],
            probe_send_sem.at[distance], probe_recv_sem.at[distance], shifted(mode=distance),
        )

    def halo_copy(local):
        return remote(
            halo_send.at[local], halo_recv.at[local],
            halo_send_sem.at[local], halo_recv_sem.at[local], shifted(tile=1),
        )

    def window_copy(index):
        return remote(
            windows.at[index], windows.at[index],
            window_send_sem.at[index], window_recv_sem.at[index], peer,
        )

    power_copy = remote(power_send, power_recv, power_sem.at[0], power_sem.at[1], peer)

    def terms_copy(index):
        local = lax.rem(index, LOCAL)
        return remote(
            terms.at[index], terms_recv.at[local],
            terms_send_sem.at[local], terms_recv_sem.at[local], peer,
        )

    def group_copy(local, distance):
        return remote(
            sums.at[local, :, group_rows(ahead(distance))], groups.at[local, distance],
            group_send_sem.at[local, distance], group_recv_sem.at[local, distance],
            shifted(mode=distance),
        )

    def rim_copy(local):
        return remote(
            rim_send.at[local], rim_recv.at[local],
            rim_send_sem.at[local], rim_recv_sem.at[local], shifted(tile=-1),
        )

    def out_copy(local, distance, place):
        return remote(
            own_part.at[local, ahead(distance)], out_ref.at[:, local, group_rows(place)],
            out_send_sem.at[local, distance], out_recv_sem.at[local, distance],
            shifted(mode=distance),
        )

    lane = lax.broadcasted_iota(jnp.int32, (8, W), 1)
    row_index = lax.broadcasted_iota(jnp.int32, (W, W), 0)

    def chosen(component, local, block):
        value = object_ref[component, local, :, 0:W]
        for index in range(1, 4):
            value = jnp.where(block == index, object_ref[component, local, :, index * W:(index + 1) * W], value)
        return value

    def block_of(first):
        return jnp.broadcast_to(((first + (W - 1) - lane) // W)[0:1], (W, W))

    for load in small_loads:
        load.wait()
    for slot in range(SLOTS):
        info_send[slot] = jnp.full((8, W), rows_ref[slot], jnp.int32)
        info_send[SLOTS + slot] = jnp.full((8, W), cols_ref[slot], jnp.int32)
    info_send[2 * SLOTS] = jnp.full((8, W), counts_ref[0], jnp.int32)
    loads[0].wait()
    sent_block = block_of(jnp.full((8, W), cols_ref[me], jnp.int32))

    def cut(local, carry):
        for component in range(2):
            halo_send[local, component] = chosen(component, local, sent_block)
        return carry

    lax.fori_loop(0, LOCAL, cut, 0)
    for load in loads[1:]:
        load.wait()
    phase = phase_ref[...].T
    turn[0] = jnp.cos(phase)
    turn[1] = jnp.sin(phase)

    pl.semaphore_wait(barrier, len(partners))
    info_copy.start()

    @pl.when(section == 0)
    def _():
        halo_copy(0).start()

    for distance in (1, 3, 2):
        probe_copy(distance).start()

    @pl.when(section == 0)
    def _():
        for local in range(1, LOCAL):
            halo_copy(local).start()

    measured_copy.start()
    info_copy.wait()
    info_load = pltpu.make_async_copy(info_recv, info_ref, load_sem.at[4])
    info_load.start()

    def build(index):
        local = lax.rem(index, LOCAL)
        halo_copy(local).wait_recv()
        block = block_of(info_recv[SLOTS + me])
        first = jnp.broadcast_to(info_recv[me][0:1], (W, W))
        for component in range(2):
            windows[index, component] = jnp.where(
                row_index >= first, halo_recv[local, component], chosen(component, local, block)
            )
        window_copy(index).start()

    def build_if_owner(index):
        @pl.when((index < SLICES) & (index // LOCAL == section))
        def _():
            build(index)

    def prepare(index):
        @pl.when(index // LOCAL != section)
        def _():
            window_copy(index).wait_recv()

        @pl.when((section == 1) & (index == 0))
        def _():
            for local in range(LOCAL):
                halo_copy(local).start()

        build_if_owner(index + 1)

    build_if_owner(0)
    info_load.wait()

    def row_of(slot):
        return info_ref[slot, 0, 0]

    def col_of(slot):
        return info_ref[SLOTS + slot, 0, 0]

    first_row, first_col = row_of(me), col_of(me)

    rows_here = me * ROW_GROUP + lax.broadcasted_iota(jnp.int32, (ROW_GROUP, W), 0)
    lanes_here = lax.broadcasted_iota(jnp.int32, (ROW_GROUP, W), 1)
    for distance in range(SLOTS):
        slot = behind(distance)
        block = (col_of(slot) + (W - 1) - lanes_here) // W
        keys_ref[distance] = jnp.where(rows_here >= row_of(slot), block + SLOTS, block)

    def place_probe(mode):
        for component in range(2):
            value = pltpu.roll(probes[mode, component], first_row, 0)
            value = pltpu.roll(value, lax.rem(first_col, W), 1)
            current[mode, :, component * W:(component + 1) * W] = value

    place_probe(0)
    for distance in (1, 3):
        probe_copy(distance).wait()
        place_probe(distance)

    forward = (tables_ref.at[0], tables_ref.at[1])
    inverse = (tables_ref.at[2], tables_ref.at[3])

    def run(waves, which):
        return stage(waves, which[0][...], which[1][...])

    def entered(index, modes):
        real, imag = windows[index, 0], windows[index, 1]
        waves = []
        for mode in modes:
            wave = current[mode]
            saved[index, mode] = wave
            waves.append(times(wave, real, imag))
        return waves

    def advance(index, modes):
        waves = [turned(wave) for wave in run(entered(index, modes), forward)]
        waves = [times(wave, turn[0], turn[1]) for wave in run(waves, forward)]
        waves = [turned(wave) for wave in run(waves, inverse)]
        waves = run(waves, inverse)
        for mode, wave in zip(modes, waves):
            current[mode] = wave

    everything = tuple(range(MODES))

    def early_step(index, carry):
        prepare(index)
        advance(index, (0, 1, 3))
        return carry

    lax.fori_loop(0, EARLY, early_step, 0)
    probe_copy(2).wait()
    place_probe(2)
    for index in range(EARLY):
        advance(index, (2,))

    def forward_step(index, carry):
        prepare(index)
        advance(index, everything)
        return carry

    lax.fori_loop(EARLY, SLICES - 1, forward_step, 0)
    prepare(SLICES - 1)
    waves = [turned(wave) for wave in run(entered(SLICES - 1, everything), forward)]
    waves = [times(wave, turn[0], turn[1]) for wave in run(waves, forward)]
    power = jnp.zeros((W, W), jnp.float32)
    for mode in range(MODES):
        far[mode] = waves[mode]
        power += waves[mode][:, :W] * waves[mode][:, :W] + waves[mode][:, W:] * waves[mode][:, W:]
    power_send[...] = power
    power_copy.start()
    measured_copy.wait()
    power_copy.wait()
    live = jnp.where(me < info_ref[2 * SLOTS, 0, 0], 2.0, 0.0).astype(jnp.float32)
    residual = live * (power_send[...] + power_recv[...] - measured_ref[...].T)
    residual = jnp.concatenate([residual, residual], axis=1)
    waves = [times_conj(residual * far[mode], turn[0], turn[1]) for mode in range(MODES)]
    waves = [turned(wave) for wave in run(waves, inverse)]
    waves = run(waves, inverse)
    for mode in range(MODES):
        current[mode] = waves[mode]

    def gather_terms(index):
        local = lax.rem(index, LOCAL)
        terms_copy(index).wait_recv()
        for component in range(2):
            sums[local, component] = terms[index, component] + terms_recv[local, component]
        for distance in (2, 1, 3):
            group_copy(local, distance).start()

    def sort_groups(index):
        local = lax.rem(index, LOCAL)
        for distance in (1, 3, 2):
            group_copy(local, distance).wait_recv()
        for component in range(2):
            groups[local, 0, component] = sums[local, component, group_rows(me)]
        keys = [keys_ref[distance] for distance in range(SLOTS)]
        def total(component, target):
            return sum(
                jnp.where(keys[distance] == target, groups[local, distance, component], 0.0)
                for distance in range(SLOTS)
            )

        for target in range(SLOTS):
            for component in range(2):
                rim_send[local, target, component] = total(component, SLOTS + target)
        rim_copy(local).start()
        for target in range(SLOTS):
            for component in range(2):
                own_part[local, target, component] = total(component, target)

    def finish(index):
        local = lax.rem(index, LOCAL)
        rim_copy(local).wait_recv()
        for target in range(SLOTS):
            for component in range(2):
                own_part[local, target, component] += rim_recv[local, target, component]
        for distance in (2, 1, 3):
            out_copy(local, distance, me).start()
        for component in range(2):
            out_ref[component, local, group_rows(me)] = own_part[local, me, component]

    def collect(index):
        total_real = jnp.zeros((W, W), jnp.float32)
        total_imag = jnp.zeros((W, W), jnp.float32)
        for mode in range(MODES):
            wave, start = current[mode], saved[index, mode]
            a, b = wave[:, :W], wave[:, W:]
            c, d = start[:, :W], start[:, W:]
            total_real += c * a + d * b
            total_imag += c * b - d * a
        terms[index, 0] = total_real
        terms[index, 1] = total_imag

    def hand_over(index):
        @pl.when(index // LOCAL != section)
        def _():
            terms_copy(index).start()

    def retreat(index):
        real, imag = windows[index, 0], windows[index, 1]
        waves = [times_conj(current[mode], real, imag) for mode in range(MODES)]
        waves = [turned(wave) for wave in run(waves, forward)]
        waves = [times_conj(wave, turn[0], turn[1]) for wave in run(waves, forward)]
        waves = [turned(wave) for wave in run(waves, inverse)]
        waves = run(waves, inverse)
        for mode in range(MODES):
            current[mode] = waves[mode]

    def deliver(index, lags):
        for lag, action in lags:
            late = index + lag

            @pl.when((late >= 0) & (late < SLICES) & (late // LOCAL == section))
            def _():
                action(late)

    late_lags = ((LAG_GATHER, sort_groups), (LAG_TERMS, gather_terms), (LAG_RIM, finish))
    lags = ((LAG_TERMS, gather_terms), (LAG_GATHER, sort_groups), (LAG_RIM, finish))

    def backward_step(step, carry):
        index = SLICES - 1 - step
        hand_over(index)
        retreat(index)
        collect(index - 1)
        deliver(index, lags)
        return carry

    collect(SLICES - 1)
    lax.fori_loop(0, SLICES - 1, backward_step, 0)
    hand_over(0)

    def drain_step(step, carry):
        deliver(-step, late_lags)
        return carry

    lax.fori_loop(0, LAG_RIM + 1, drain_step, 0)

    for distance in (1, 3, 2):
        for local in range(LOCAL):
            out_copy(local, distance, behind(distance)).wait_recv()

    def drain(local, carry):
        halo_copy(local).wait_send()
        window_copy(section * LOCAL + local).wait_send()
        terms_copy((1 - section) * LOCAL + local).wait_send()
        rim_copy(local).wait_send()
        for distance in (1, 2, 3):
            group_copy(local, distance).wait_send()
            out_copy(local, distance, me).wait_send()
        return carry

    lax.fori_loop(0, LOCAL, drain, 0)


def body(object_slices, probe_modes, propagator_phase, measured, row_offset, col_offset, counts):
    square = (W, W)
    vmem = lambda *shape: pltpu.VMEM(shape, jnp.float32)
    dma = lambda *shape: pltpu.SemaphoreType.DMA(shape)
    smem_spec = pl.BlockSpec(memory_space=pltpu.SMEM)
    vmem_spec = pl.BlockSpec(memory_space=pltpu.VMEM)
    hbm_spec = pl.BlockSpec(memory_space=pltpu.HBM)
    operands = (
        row_offset, col_offset, counts, probe_modes, object_slices, propagator_phase, measured,
        jnp.asarray(tables()),
    )
    operands = [
        operand if operand is counts else pltpu.with_memory_space_constraint(operand, pltpu.HBM)
        for operand in operands
    ]
    return pl.pallas_call(
        kernel,
        out_shape=jax.ShapeDtypeStruct((2, LOCAL) + square, jnp.float32),
        in_specs=[hbm_spec] * 2 + [smem_spec] + [hbm_spec] * 5,
        out_specs=vmem_spec,
        scratch_shapes=[
            pltpu.SMEM((SLOTS,), jnp.int32), pltpu.SMEM((SLOTS,), jnp.int32),
            vmem(*object_slices.shape), vmem(*square), vmem(*square),
            pltpu.VMEM((4, 2 * W, 2 * W), jnp.bfloat16),
            pltpu.VMEM((2 * SLOTS + 1, 8, W), jnp.int32), pltpu.VMEM((2 * SLOTS + 1, 8, W), jnp.int32),
            pltpu.SMEM((2 * SLOTS + 1, 8, W), jnp.int32),
            pltpu.VMEM((SLOTS, ROW_GROUP, W), jnp.int32),
            vmem(MODES, 2, *square),
            vmem(LOCAL, 2, *square), vmem(LOCAL, 2, *square),
            vmem(SLICES, 2, *square),
            vmem(SLICES, MODES, W, 2 * W),
            vmem(2, *square),
            vmem(MODES, W, 2 * W), vmem(MODES, W, 2 * W),
            vmem(*square), vmem(*square),
            vmem(SLICES, 2, *square), vmem(LOCAL, 2, *square),
            vmem(LOCAL, 2, *square),
            vmem(LOCAL, SLOTS, 2, ROW_GROUP, W),
            vmem(LOCAL, SLOTS, 2, ROW_GROUP, W), vmem(LOCAL, SLOTS, 2, ROW_GROUP, W),
            vmem(LOCAL, SLOTS, 2, ROW_GROUP, W),
            dma(2), dma(5), dma(2), dma(2), dma(4), dma(4), dma(LOCAL), dma(LOCAL),
            dma(SLICES), dma(SLICES), dma(2), dma(LOCAL), dma(LOCAL),
            dma(LOCAL, SLOTS), dma(LOCAL, SLOTS), dma(LOCAL), dma(LOCAL),
            dma(LOCAL, SLOTS), dma(LOCAL, SLOTS),
        ],
        compiler_params=pltpu.CompilerParams(
            collective_id=0, has_side_effects=True, vmem_limit_bytes=40 * 1024 * 1024
        ),
    )(*operands)


def solution(mesh):
    in_specs = (
        P(None, "section", "tile", None),
        P(None, "mode", None, None),
        P(),
        P("tile", None, None),
        P("tile"),
        P("tile"),
        P("tile"),
    )
    out_specs = P(None, "section", "tile", "mode")
    return jax.shard_map(body, mesh=mesh, in_specs=in_specs, out_specs=out_specs, check_vma=False)
```

```python
import functools
import math

import jax
import jax.numpy as jnp
import ml_dtypes
import numpy as np
from jax import lax
from jax.experimental import pallas as pl
from jax.experimental.pallas import tpu as pltpu
from jax.sharding import PartitionSpec as P

W = 128
SLICES = 8
LOCAL = 4
MODES = 4
SLOTS = 4
INFO = 16
EARLY = 0
MEASURED_STEP = 3
ROW_GROUP = 32
LAG_TERMS = 0
LAG_GATHER = 3
LAG_RIM = 7
MESH = pl.DeviceIdType.MESH


def tables():
    points = np.arange(W)
    angles = (points[:, None] * points[None, :] % W) * (-2.0 * math.pi / W)
    cos_table = np.cos(angles) / math.sqrt(W)
    sin_table = np.sin(angles) / math.sqrt(W)
    forward = np.block([[cos_table, sin_table], [-sin_table, cos_table]]).astype(np.float32)
    parts = []
    for table in (forward, forward.T):
        high = table.astype(ml_dtypes.bfloat16)
        parts += [high, (table - high.astype(np.float32)).astype(ml_dtypes.bfloat16)]
    return np.stack(parts)


def shifted(**steps):
    place = {}
    for axis, step in steps.items():
        size = lax.axis_size(axis)
        place[axis] = lax.rem(lax.axis_index(axis) + (step + size), size)
    return place


def dot(left, right):
    return jnp.dot(left, right, preferred_element_type=jnp.float32)


def stage(waves, high_table, low_table):
    out = []
    for wave in waves:
        high = wave.astype(jnp.bfloat16)
        low = (wave - high.astype(jnp.float32)).astype(jnp.bfloat16)
        out.append(dot(high, high_table) + dot(low, high_table) + dot(high, low_table))
    return out


def times(wave, real, imag):
    a, b = wave[:, :W], wave[:, W:]
    return jnp.concatenate([a * real - b * imag, a * imag + b * real], axis=1)


def times_conj(wave, real, imag):
    a, b = wave[:, :W], wave[:, W:]
    return jnp.concatenate([a * real + b * imag, b * real - a * imag], axis=1)


def turned(wave):
    return jnp.concatenate([wave[:, :W].T, wave[:, W:].T], axis=1)


def kernel(
    rows_hbm, cols_hbm, counts_ref, probe_hbm, object_hbm, phase_hbm, measured_hbm, tables_hbm,
    out_ref,
    rows_ref, cols_ref, object_ref, phase_ref, measured_ref, tables_ref,
    info_send, info_recv, info_ref, keys_ref, probes, halo_send, halo_recv, windows, saved, turn, far, current,
    power_send, power_recv, terms, terms_recv, sums, groups, rim_send, rim_recv, own_part,
    small_sem, load_sem, info_sem, measured_sem, probe_send_sem, probe_recv_sem, halo_send_sem, halo_recv_sem,
    window_send_sem, window_recv_sem, power_sem, terms_send_sem, terms_recv_sem,
    group_send_sem, group_recv_sem, rim_send_sem, rim_recv_sem, out_send_sem, out_recv_sem,
):
    section = lax.axis_index("section")
    me = lax.axis_index("mode")
    peer = shifted(section=1)

    barrier = pltpu.get_barrier_semaphore()
    partners = [shifted(tile=-1), shifted(tile=1), shifted(mode=2), shifted(mode=1), shifted(mode=3), peer]
    for partner in partners:
        pl.semaphore_signal(barrier, 1, device_id=partner, device_id_type=MESH)

    loads = [
        pltpu.make_async_copy(object_hbm, object_ref, load_sem.at[0]),
        pltpu.make_async_copy(phase_hbm, phase_ref, load_sem.at[1]),
        pltpu.make_async_copy(tables_hbm, tables_ref, load_sem.at[2]),
        pltpu.make_async_copy(probe_hbm.at[:, section], probes.at[0], load_sem.at[3]),
    ]
    small_loads = [
        pltpu.make_async_copy(source, target, small_sem.at[index])
        for index, (source, target) in enumerate(
            ((rows_hbm, rows_ref), (cols_hbm, cols_ref))
        )
    ]
    for load in small_loads + loads:
        load.start()

    def remote(source, target, send_sem, recv_sem, device):
        return pltpu.make_async_remote_copy(
            src_ref=source, dst_ref=target, send_sem=send_sem, recv_sem=recv_sem,
            device_id=device, device_id_type=MESH,
        )

    def behind(distance):
        return lax.rem(me + (SLOTS - distance), SLOTS)

    def ahead(distance):
        return lax.rem(me + distance, SLOTS)

    def group_rows(index):
        return pl.ds(pl.multiple_of(index * ROW_GROUP, ROW_GROUP), ROW_GROUP)

    info_copy = remote(info_send, info_recv, info_sem.at[0], info_sem.at[1], shifted(tile=1))
    measured_copy = remote(
        measured_hbm.at[me], measured_ref, measured_sem.at[0], measured_sem.at[1], shifted(tile=1)
    )

    def probe_copy(distance):
        return remote(
            probe_hbm.at[:, section], probes.at[distance],
            probe_send_sem.at[distance], probe_recv_sem.at[distance], shifted(mode=distance),
        )

    def halo_copy(local):
        return remote(
            halo_send.at[local], halo_recv.at[local],
            halo_send_sem.at[local], halo_recv_sem.at[local], shifted(tile=1),
        )

    def window_copy(index):
        return remote(
            windows.at[index], windows.at[index],
            window_send_sem.at[index], window_recv_sem.at[index], peer,
        )

    power_copy = remote(power_send, power_recv, power_sem.at[0], power_sem.at[1], peer)

    def terms_copy(index):
        local = lax.rem(index, LOCAL)
        return remote(
            terms.at[index], terms_recv.at[local],
            terms_send_sem.at[local], terms_recv_sem.at[local], peer,
        )

    def group_copy(local, distance):
        return remote(
            sums.at[local, :, group_rows(ahead(distance))], groups.at[local, distance],
            group_send_sem.at[local, distance], group_recv_sem.at[local, distance],
            shifted(mode=distance),
        )

    def rim_copy(local):
        return remote(
            rim_send.at[local], rim_recv.at[local],
            rim_send_sem.at[local], rim_recv_sem.at[local], shifted(tile=-1),
        )

    def out_copy(local, distance, place):
        return remote(
            own_part.at[local, ahead(distance)], out_ref.at[:, local, group_rows(place)],
            out_send_sem.at[local, distance], out_recv_sem.at[local, distance],
            shifted(mode=distance),
        )

    lane = lax.broadcasted_iota(jnp.int32, (1, W), 1)
    row_index = lax.broadcasted_iota(jnp.int32, (W, W), 0)

    def chosen(component, local, block):
        value = object_ref[component, local, :, 0:W]
        for index in range(1, 4):
            value = jnp.where(block == index, object_ref[component, local, :, index * W:(index + 1) * W], value)
        return value

    def block_of(first):
        return jnp.broadcast_to((first + (W - 1) - lane) // W, (W, W))

    for load in small_loads:
        load.wait()
    rank = lax.broadcasted_iota(jnp.int32, (INFO, W), 0)
    info = jnp.full((INFO, W), counts_ref[0], jnp.int32)
    for slot in range(SLOTS):
        info = jnp.where(rank == slot, rows_ref[slot], info)
        info = jnp.where(rank == SLOTS + slot, cols_ref[slot], info)
    info_send[...] = info
    loads[0].wait()
    sent_block = block_of(jnp.full((1, W), cols_ref[me], jnp.int32))

    def cut(local, carry):
        for component in range(2):
            halo_send[local, component] = chosen(component, local, sent_block)
        return carry

    lax.fori_loop(0, LOCAL, cut, 0)
    for load in loads[1:]:
        load.wait()
    phase = phase_ref[...].T
    turn[0] = jnp.cos(phase)
    turn[1] = jnp.sin(phase)

    pl.semaphore_wait(barrier, len(partners))
    info_copy.start()

    @pl.when(section == 0)
    def _():
        halo_copy(0).start()

    for distance in (1, 3, 2):
        probe_copy(distance).start()

    @pl.when(section == 0)
    def _():
        for local in range(1, LOCAL):
            halo_copy(local).start()

    info_copy.wait()
    info_load = pltpu.make_async_copy(info_recv, info_ref, load_sem.at[4])
    info_load.start()

    def build(index):
        local = lax.rem(index, LOCAL)
        halo_copy(local).wait_recv()
        block = block_of(info_recv[pl.ds(SLOTS + me, 1)])
        first = jnp.broadcast_to(info_recv[pl.ds(me, 1)], (W, W))
        for component in range(2):
            windows[index, component] = jnp.where(
                row_index >= first, halo_recv[local, component], chosen(component, local, block)
            )
        window_copy(index).start()

    def build_if_owner(index):
        @pl.when((index < SLICES) & (index // LOCAL == section))
        def _():
            build(index)

    def prepare(index):
        @pl.when(index // LOCAL != section)
        def _():
            window_copy(index).wait_recv()

        @pl.when((section == 1) & (index < 2))
        def _():
            for local in range(2):
                halo_copy(2 * index + local).start()

        @pl.when(index == MEASURED_STEP)
        def _():
            measured_copy.start()

        build_if_owner(index + 1)

    build_if_owner(0)
    info_load.wait()

    def row_of(slot):
        return info_ref[slot, 0]

    def col_of(slot):
        return info_ref[SLOTS + slot, 0]

    first_row, first_col = row_of(me), col_of(me)

    rows_here = me * ROW_GROUP + lax.broadcasted_iota(jnp.int32, (ROW_GROUP, W), 0)
    lanes_here = lax.broadcasted_iota(jnp.int32, (ROW_GROUP, W), 1)
    for distance in range(SLOTS):
        slot = behind(distance)
        block = (col_of(slot) + (W - 1) - lanes_here) // W
        keys_ref[distance] = jnp.where(rows_here >= row_of(slot), block + SLOTS, block)

    def place_probe(mode):
        for component in range(2):
            value = pltpu.roll(probes[mode, component], first_row, 0)
            value = pltpu.roll(value, lax.rem(first_col, W), 1)
            current[mode, :, component * W:(component + 1) * W] = value

    place_probe(0)
    for distance in (1, 3):
        probe_copy(distance).wait()
        place_probe(distance)

    forward = (tables_ref.at[0], tables_ref.at[1])
    inverse = (tables_ref.at[2], tables_ref.at[3])

    def run(waves, which):
        return stage(waves, which[0][...], which[1][...])

    def entered(index, modes):
        real, imag = windows[index, 0], windows[index, 1]
        waves = []
        for mode in modes:
            wave = current[mode]
            saved[index, mode] = wave
            waves.append(times(wave, real, imag))
        return waves

    def advance(index, modes):
        waves = [turned(wave) for wave in run(entered(index, modes), forward)]
        waves = [times(wave, turn[0], turn[1]) for wave in run(waves, forward)]
        waves = [turned(wave) for wave in run(waves, inverse)]
        waves = run(waves, inverse)
        for mode, wave in zip(modes, waves):
            current[mode] = wave

    everything = tuple(range(MODES))

    def early_step(index, carry):
        prepare(index)
        advance(index, (0, 1, 3))
        return carry

    lax.fori_loop(0, EARLY, early_step, 0)
    probe_copy(2).wait()
    place_probe(2)
    for index in range(EARLY):
        advance(index, (2,))

    def forward_step(index, carry):
        prepare(index)
        advance(index, everything)
        return carry

    lax.fori_loop(EARLY, SLICES - 1, forward_step, 0)
    prepare(SLICES - 1)
    waves = [turned(wave) for wave in run(entered(SLICES - 1, everything), forward)]
    waves = [times(wave, turn[0], turn[1]) for wave in run(waves, forward)]
    power = jnp.zeros((W, W), jnp.float32)
    for mode in range(MODES):
        far[mode] = waves[mode]
        power += waves[mode][:, :W] * waves[mode][:, :W] + waves[mode][:, W:] * waves[mode][:, W:]
    power_send[...] = power
    power_copy.start()
    measured_copy.wait()
    power_copy.wait()
    live = jnp.where(me < info_ref[2 * SLOTS, 0], 2.0, 0.0).astype(jnp.float32)
    residual = live * (power_send[...] + power_recv[...] - measured_ref[...].T)
    residual = jnp.concatenate([residual, residual], axis=1)
    waves = [times_conj(residual * far[mode], turn[0], turn[1]) for mode in range(MODES)]
    waves = [turned(wave) for wave in run(waves, inverse)]
    waves = run(waves, inverse)
    for mode in range(MODES):
        current[mode] = waves[mode]

    def gather_terms(index):
        local = lax.rem(index, LOCAL)
        terms_copy(index).wait_recv()
        for component in range(2):
            sums[local, component] = terms[index, component] + terms_recv[local, component]
        for distance in (2, 1, 3):
            group_copy(local, distance).start()

    def sort_groups(index):
        local = lax.rem(index, LOCAL)
        for distance in (1, 3, 2):
            group_copy(local, distance).wait_recv()
        for component in range(2):
            groups[local, 0, component] = sums[local, component, group_rows(me)]
        keys = [keys_ref[distance] for distance in range(SLOTS)]
        def total(component, target):
            return sum(
                jnp.where(keys[distance] == target, groups[local, distance, component], 0.0)
                for distance in range(SLOTS)
            )

        for target in range(SLOTS):
            for component in range(2):
                rim_send[local, target, component] = total(component, SLOTS + target)
        rim_copy(local).start()
        for target in range(SLOTS):
            for component in range(2):
                own_part[local, target, component] = total(component, target)

    def finish(index):
        local = lax.rem(index, LOCAL)
        rim_copy(local).wait_recv()
        for target in range(SLOTS):
            for component in range(2):
                own_part[local, target, component] += rim_recv[local, target, component]
        for distance in (2, 1, 3):
            out_copy(local, distance, me).start()
        for component in range(2):
            out_ref[component, local, group_rows(me)] = own_part[local, me, component]

    def collect(index):
        total_real = jnp.zeros((W, W), jnp.float32)
        total_imag = jnp.zeros((W, W), jnp.float32)
        for mode in range(MODES):
            wave, start = current[mode], saved[index, mode]
            a, b = wave[:, :W], wave[:, W:]
            c, d = start[:, :W], start[:, W:]
            total_real += c * a + d * b
            total_imag += c * b - d * a
        terms[index, 0] = total_real
        terms[index, 1] = total_imag

    def hand_over(index):
        @pl.when(index // LOCAL != section)
        def _():
            terms_copy(index).start()

    def retreat(index):
        real, imag = windows[index, 0], windows[index, 1]
        waves = [times_conj(current[mode], real, imag) for mode in range(MODES)]
        waves = [turned(wave) for wave in run(waves, forward)]
        waves = [times_conj(wave, turn[0], turn[1]) for wave in run(waves, forward)]
        waves = [turned(wave) for wave in run(waves, inverse)]
        waves = run(waves, inverse)
        for mode in range(MODES):
            current[mode] = waves[mode]

    def deliver(index, lags):
        for lag, action in lags:
            late = index + lag

            @pl.when((late >= 0) & (late < SLICES) & (late // LOCAL == section))
            def _():
                action(late)

    late_lags = ((LAG_GATHER, sort_groups), (LAG_TERMS, gather_terms), (LAG_RIM, finish))
    lags = ((LAG_TERMS, gather_terms), (LAG_GATHER, sort_groups), (LAG_RIM, finish))

    def backward_step(step, carry):
        index = SLICES - 1 - step
        hand_over(index)
        retreat(index)
        collect(index - 1)
        deliver(index, lags)
        return carry

    collect(SLICES - 1)
    lax.fori_loop(0, SLICES - 1, backward_step, 0)
    hand_over(0)

    def drain_step(step, carry):
        deliver(-step, late_lags)
        return carry

    lax.fori_loop(0, LAG_RIM + 1, drain_step, 0)

    for distance in (1, 3, 2):
        for local in range(LOCAL):
            out_copy(local, distance, behind(distance)).wait_recv()

    def drain(local, carry):
        halo_copy(local).wait_send()
        window_copy(section * LOCAL + local).wait_send()
        terms_copy((1 - section) * LOCAL + local).wait_send()
        rim_copy(local).wait_send()
        for distance in (1, 2, 3):
            group_copy(local, distance).wait_send()
            out_copy(local, distance, me).wait_send()
        return carry

    lax.fori_loop(0, LOCAL, drain, 0)


def body(object_slices, probe_modes, propagator_phase, measured, row_offset, col_offset, counts):
    square = (W, W)
    vmem = lambda *shape: pltpu.VMEM(shape, jnp.float32)
    dma = lambda *shape: pltpu.SemaphoreType.DMA(shape)
    smem_spec = pl.BlockSpec(memory_space=pltpu.SMEM)
    vmem_spec = pl.BlockSpec(memory_space=pltpu.VMEM)
    hbm_spec = pl.BlockSpec(memory_space=pltpu.HBM)
    operands = (
        row_offset, col_offset, counts, probe_modes, object_slices, propagator_phase, measured,
        jnp.asarray(tables()),
    )
    operands = [
        operand if operand is counts else pltpu.with_memory_space_constraint(operand, pltpu.HBM)
        for operand in operands
    ]
    return pl.pallas_call(
        kernel,
        out_shape=jax.ShapeDtypeStruct((2, LOCAL) + square, jnp.float32),
        in_specs=[hbm_spec] * 2 + [smem_spec] + [hbm_spec] * 5,
        out_specs=vmem_spec,
        scratch_shapes=[
            pltpu.SMEM((SLOTS,), jnp.int32), pltpu.SMEM((SLOTS,), jnp.int32),
            vmem(*object_slices.shape), vmem(*square), vmem(*square),
            pltpu.VMEM((4, 2 * W, 2 * W), jnp.bfloat16),
            pltpu.VMEM((INFO, W), jnp.int32), pltpu.VMEM((INFO, W), jnp.int32),
            pltpu.SMEM((INFO, W), jnp.int32),
            pltpu.VMEM((SLOTS, ROW_GROUP, W), jnp.int32),
            vmem(MODES, 2, *square),
            vmem(LOCAL, 2, *square), vmem(LOCAL, 2, *square),
            vmem(SLICES, 2, *square),
            vmem(SLICES, MODES, W, 2 * W),
            vmem(2, *square),
            vmem(MODES, W, 2 * W), vmem(MODES, W, 2 * W),
            vmem(*square), vmem(*square),
            vmem(SLICES, 2, *square), vmem(LOCAL, 2, *square),
            vmem(LOCAL, 2, *square),
            vmem(LOCAL, SLOTS, 2, ROW_GROUP, W),
            vmem(LOCAL, SLOTS, 2, ROW_GROUP, W), vmem(LOCAL, SLOTS, 2, ROW_GROUP, W),
            vmem(LOCAL, SLOTS, 2, ROW_GROUP, W),
            dma(2), dma(5), dma(2), dma(2), dma(4), dma(4), dma(LOCAL), dma(LOCAL),
            dma(SLICES), dma(SLICES), dma(2), dma(LOCAL), dma(LOCAL),
            dma(LOCAL, SLOTS), dma(LOCAL, SLOTS), dma(LOCAL), dma(LOCAL),
            dma(LOCAL, SLOTS), dma(LOCAL, SLOTS),
        ],
        compiler_params=pltpu.CompilerParams(
            collective_id=0, has_side_effects=True, vmem_limit_bytes=40 * 1024 * 1024
        ),
    )(*operands)


def solution(mesh):
    in_specs = (
        P(None, "section", "tile", None),
        P(None, "mode", None, None),
        P(),
        P("tile", None, None),
        P("tile"),
        P("tile"),
        P("tile"),
    )
    out_specs = P(None, "section", "tile", "mode")
    return jax.shard_map(body, mesh=mesh, in_specs=in_specs, out_specs=out_specs, check_vma=False)
```

```python
import functools
import math

import jax
import jax.numpy as jnp
import ml_dtypes
import numpy as np
from jax import lax
from jax.experimental import pallas as pl
from jax.experimental.pallas import tpu as pltpu
from jax.sharding import PartitionSpec as P

W = 128
SLICES = 8
LOCAL = 4
MODES = 4
SLOTS = 4
INFO = 16
EARLY = 0
MEASURED_STEP = 3
ROW_GROUP = 32
LAG_TERMS = 0
LAG_GATHER = 3
LAG_RIM = 7
MESH = pl.DeviceIdType.MESH


def tables():
    points = np.arange(W)
    angles = (points[:, None] * points[None, :] % W) * (-2.0 * math.pi / W)
    cos_table = np.cos(angles) / math.sqrt(W)
    sin_table = np.sin(angles) / math.sqrt(W)
    forward = np.block([[cos_table, sin_table], [-sin_table, cos_table]]).astype(np.float32)
    parts = []
    for table in (forward, forward.T):
        high = table.astype(ml_dtypes.bfloat16)
        parts += [high, (table - high.astype(np.float32)).astype(ml_dtypes.bfloat16)]
    return np.stack(parts)


def shifted(**steps):
    place = {}
    for axis, step in steps.items():
        size = lax.axis_size(axis)
        place[axis] = lax.rem(lax.axis_index(axis) + (step + size), size)
    return place


def dot(left, right):
    return jnp.dot(left, right, preferred_element_type=jnp.float32)


def stage(waves, high_table, low_table):
    out = []
    for wave in waves:
        high = wave.astype(jnp.bfloat16)
        low = (wave - high.astype(jnp.float32)).astype(jnp.bfloat16)
        out.append(dot(high, high_table) + dot(low, high_table) + dot(high, low_table))
    return out


def times(wave, real, imag):
    a, b = wave[:, :W], wave[:, W:]
    return jnp.concatenate([a * real - b * imag, a * imag + b * real], axis=1)


def times_conj(wave, real, imag):
    a, b = wave[:, :W], wave[:, W:]
    return jnp.concatenate([a * real + b * imag, b * real - a * imag], axis=1)


def turned(wave):
    return jnp.concatenate([wave[:, :W].T, wave[:, W:].T], axis=1)


def kernel(
    rows_hbm, cols_hbm, counts_ref, probe_hbm, object_hbm, phase_hbm, measured_hbm, tables_hbm,
    out_ref,
    rows_ref, cols_ref, object_ref, phase_ref, measured_ref, tables_ref,
    info_send, info_recv, info_ref, keys_ref, probes, halo_send, halo_recv, windows, saved, turn, far, current,
    power_send, power_recv, terms, terms_recv, sums, groups, rim_send, rim_recv, own_part,
    small_sem, load_sem, info_sem, measured_sem, probe_send_sem, probe_recv_sem, halo_send_sem, halo_recv_sem,
    window_send_sem, window_recv_sem, power_sem, terms_send_sem, terms_recv_sem,
    group_send_sem, group_recv_sem, rim_send_sem, rim_recv_sem, out_send_sem, out_recv_sem,
):
    section = lax.axis_index("section")
    me = lax.axis_index("mode")
    peer = shifted(section=1)

    barrier = pltpu.get_barrier_semaphore()
    partners = [shifted(tile=-1), shifted(tile=1), shifted(mode=2), shifted(mode=1), shifted(mode=3), peer]
    for partner in partners:
        pl.semaphore_signal(barrier, 1, device_id=partner, device_id_type=MESH)

    loads = [
        pltpu.make_async_copy(object_hbm, object_ref, load_sem.at[0]),
        pltpu.make_async_copy(phase_hbm, phase_ref, load_sem.at[1]),
        pltpu.make_async_copy(tables_hbm, tables_ref, load_sem.at[2]),
        pltpu.make_async_copy(probe_hbm.at[:, section], probes.at[0], load_sem.at[3]),
    ]
    small_loads = [
        pltpu.make_async_copy(source, target, small_sem.at[index])
        for index, (source, target) in enumerate(
            ((rows_hbm, rows_ref), (cols_hbm, cols_ref))
        )
    ]
    for load in small_loads + loads:
        load.start()

    def remote(source, target, send_sem, recv_sem, device):
        return pltpu.make_async_remote_copy(
            src_ref=source, dst_ref=target, send_sem=send_sem, recv_sem=recv_sem,
            device_id=device, device_id_type=MESH,
        )

    def behind(distance):
        return lax.rem(me + (SLOTS - distance), SLOTS)

    def ahead(distance):
        return lax.rem(me + distance, SLOTS)

    def group_rows(index):
        return pl.ds(pl.multiple_of(index * ROW_GROUP, ROW_GROUP), ROW_GROUP)

    info_copy = remote(info_send, info_recv, info_sem.at[0], info_sem.at[1], shifted(tile=1))
    measured_copy = remote(
        measured_hbm.at[me], measured_ref, measured_sem.at[0], measured_sem.at[1], shifted(tile=1)
    )

    def probe_copy(distance):
        return remote(
            probe_hbm.at[:, section], probes.at[distance],
            probe_send_sem.at[distance], probe_recv_sem.at[distance], shifted(mode=distance),
        )

    def halo_copy(local):
        return remote(
            halo_send.at[local], halo_recv.at[local],
            halo_send_sem.at[local], halo_recv_sem.at[local], shifted(tile=1),
        )

    def window_copy(index):
        return remote(
            windows.at[index], windows.at[index],
            window_send_sem.at[index], window_recv_sem.at[index], peer,
        )

    power_copy = remote(power_send, power_recv, power_sem.at[0], power_sem.at[1], peer)

    def terms_copy(index):
        local = lax.rem(index, LOCAL)
        return remote(
            terms.at[index], terms_recv.at[local],
            terms_send_sem.at[local], terms_recv_sem.at[local], peer,
        )

    def group_copy(local, distance):
        return remote(
            sums.at[local, :, group_rows(ahead(distance))], groups.at[local, distance],
            group_send_sem.at[local, distance], group_recv_sem.at[local, distance],
            shifted(mode=distance),
        )

    def rim_copy(local):
        return remote(
            rim_send.at[local], rim_recv.at[local],
            rim_send_sem.at[local], rim_recv_sem.at[local], shifted(tile=-1),
        )

    def out_copy(local, distance, place):
        return remote(
            own_part.at[local, ahead(distance)], out_ref.at[:, local, group_rows(place)],
            out_send_sem.at[local, distance], out_recv_sem.at[local, distance],
            shifted(mode=distance),
        )

    lane = lax.broadcasted_iota(jnp.int32, (1, W), 1)
    row_index = lax.broadcasted_iota(jnp.int32, (W, W), 0)

    def chosen(component, local, block):
        value = object_ref[component, local, :, 0:W]
        for index in range(1, 4):
            value = jnp.where(block == index, object_ref[component, local, :, index * W:(index + 1) * W], value)
        return value

    def block_of(first):
        return jnp.broadcast_to((first + (W - 1) - lane) // W, (W, W))

    for load in small_loads:
        load.wait()
    rank = lax.broadcasted_iota(jnp.int32, (INFO, W), 0)
    info = jnp.full((INFO, W), counts_ref[0], jnp.int32)
    for slot in range(SLOTS):
        info = jnp.where(rank == slot, rows_ref[slot], info)
        info = jnp.where(rank == SLOTS + slot, cols_ref[slot], info)
    info_send[...] = info
    loads[0].wait()
    sent_block = block_of(jnp.full((1, W), cols_ref[me], jnp.int32))

    def cut(local, carry):
        for component in range(2):
            halo_send[local, component] = chosen(component, local, sent_block)
        return carry

    lax.fori_loop(0, LOCAL, cut, 0)
    for load in loads[1:]:
        load.wait()
    phase = phase_ref[...].T
    turn[0] = jnp.cos(phase)
    turn[1] = jnp.sin(phase)

    pl.semaphore_wait(barrier, len(partners))
    info_copy.start()

    @pl.when(section == 0)
    def _():
        halo_copy(0).start()

    for distance in (1, 3, 2):
        probe_copy(distance).start()

    @pl.when(section == 0)
    def _():
        for local in range(1, LOCAL):
            halo_copy(local).start()

    info_copy.wait()
    info_load = pltpu.make_async_copy(info_recv, info_ref, load_sem.at[4])
    info_load.start()

    def build(index):
        local = lax.rem(index, LOCAL)
        halo_copy(local).wait_recv()
        block = block_of(info_recv[pl.ds(SLOTS + me, 1)])
        first = jnp.broadcast_to(info_recv[pl.ds(me, 1)], (W, W))
        for component in range(2):
            windows[index, component] = jnp.where(
                row_index >= first, halo_recv[local, component], chosen(component, local, block)
            )
        window_copy(index).start()

    def build_if_owner(index):
        @pl.when((index < SLICES) & (index // LOCAL == section))
        def _():
            build(index)

    def prepare(index):
        @pl.when(index // LOCAL != section)
        def _():
            window_copy(index).wait_recv()

        @pl.when((section == 1) & (index < 2))
        def _():
            for local in range(2):
                halo_copy(2 * index + local).start()

        @pl.when(index == MEASURED_STEP)
        def _():
            measured_copy.start()

        build_if_owner(index + 1)

    build_if_owner(0)
    info_load.wait()

    def row_of(slot):
        return info_ref[slot, 0]

    def col_of(slot):
        return info_ref[SLOTS + slot, 0]

    first_row, first_col = row_of(me), col_of(me)

    rows_here = me * ROW_GROUP + lax.broadcasted_iota(jnp.int32, (ROW_GROUP, W), 0)
    lanes_here = lax.broadcasted_iota(jnp.int32, (ROW_GROUP, W), 1)
    for distance in range(SLOTS):
        slot = behind(distance)
        block = (col_of(slot) + (W - 1) - lanes_here) // W
        keys_ref[distance] = jnp.where(rows_here >= row_of(slot), block + SLOTS, block)

    def place_probe(mode):
        for component in range(2):
            value = pltpu.roll(probes[mode, component], first_row, 0)
            value = pltpu.roll(value, lax.rem(first_col, W), 1)
            current[mode, :, component * W:(component + 1) * W] = value

    place_probe(0)
    for distance in (1, 3):
        probe_copy(distance).wait()
        place_probe(distance)

    forward = (tables_ref.at[0], tables_ref.at[1])
    inverse = (tables_ref.at[2], tables_ref.at[3])

    def run(waves, which):
        return stage(waves, which[0][...], which[1][...])

    def entered(index, modes):
        real, imag = windows[index, 0], windows[index, 1]
        waves = []
        for mode in modes:
            wave = current[mode]
            saved[index, mode] = wave
            waves.append(times(wave, real, imag))
        return waves

    def advance(index, modes):
        waves = [turned(wave) for wave in run(entered(index, modes), forward)]
        waves = [times(wave, turn[0], turn[1]) for wave in run(waves, forward)]
        waves = [turned(wave) for wave in run(waves, inverse)]
        waves = run(waves, inverse)
        for mode, wave in zip(modes, waves):
            current[mode] = wave

    everything = tuple(range(MODES))

    def early_step(index, carry):
        prepare(index)
        advance(index, (0, 1, 3))
        return carry

    lax.fori_loop(0, EARLY, early_step, 0)
    probe_copy(2).wait()
    place_probe(2)
    for index in range(EARLY):
        advance(index, (2,))

    def forward_step(index, carry):
        prepare(index)
        advance(index, everything)
        return carry

    lax.fori_loop(EARLY, SLICES - 1, forward_step, 0)
    prepare(SLICES - 1)
    waves = [turned(wave) for wave in run(entered(SLICES - 1, everything), forward)]
    waves = [times(wave, turn[0], turn[1]) for wave in run(waves, forward)]
    power = jnp.zeros((W, W), jnp.float32)
    for mode in range(MODES):
        far[mode] = waves[mode]
        power += waves[mode][:, :W] * waves[mode][:, :W] + waves[mode][:, W:] * waves[mode][:, W:]
    power_send[...] = power
    power_copy.start()
    measured_copy.wait()
    power_copy.wait()
    live = jnp.where(me < info_ref[2 * SLOTS, 0], 2.0, 0.0).astype(jnp.float32)
    residual = live * (power_send[...] + power_recv[...] - measured_ref[...].T)
    residual = jnp.concatenate([residual, residual], axis=1)
    waves = [times_conj(residual * far[mode], turn[0], turn[1]) for mode in range(MODES)]
    waves = [turned(wave) for wave in run(waves, inverse)]
    waves = run(waves, inverse)
    for mode in range(MODES):
        current[mode] = waves[mode]

    def gather_terms(index):
        local = lax.rem(index, LOCAL)
        terms_copy(index).wait_recv()
        for distance in (2, 1, 3, 0):
            rows = group_rows(ahead(distance))
            for component in range(2):
                sums[local, component, rows] = terms[index, component, rows] + terms_recv[local, component, rows]
            if distance:
                group_copy(local, distance).start()

    def sort_groups(index):
        local = lax.rem(index, LOCAL)
        for distance in (1, 3, 2):
            group_copy(local, distance).wait_recv()
        for component in range(2):
            groups[local, 0, component] = sums[local, component, group_rows(me)]
        keys = [keys_ref[distance] for distance in range(SLOTS)]
        def total(component, target):
            return sum(
                jnp.where(keys[distance] == target, groups[local, distance, component], 0.0)
                for distance in range(SLOTS)
            )

        for target in range(SLOTS):
            for component in range(2):
                rim_send[local, target, component] = total(component, SLOTS + target)
        rim_copy(local).start()
        for target in range(SLOTS):
            for component in range(2):
                own_part[local, target, component] = total(component, target)

    def finish(index):
        local = lax.rem(index, LOCAL)
        rim_copy(local).wait_recv()
        for target in range(SLOTS):
            for component in range(2):
                own_part[local, target, component] += rim_recv[local, target, component]
        for distance in (2, 1, 3):
            out_copy(local, distance, me).start()
        for component in range(2):
            out_ref[component, local, group_rows(me)] = own_part[local, me, component]

    def collect(index):
        total_real = jnp.zeros((W, W), jnp.float32)
        total_imag = jnp.zeros((W, W), jnp.float32)
        for mode in range(MODES):
            wave, start = current[mode], saved[index, mode]
            a, b = wave[:, :W], wave[:, W:]
            c, d = start[:, :W], start[:, W:]
            total_real += c * a + d * b
            total_imag += c * b - d * a
        terms[index, 0] = total_real
        terms[index, 1] = total_imag

    def hand_over(index):
        @pl.when(index // LOCAL != section)
        def _():
            terms_copy(index).start()

    def retreat(index):
        real, imag = windows[index, 0], windows[index, 1]
        waves = [times_conj(current[mode], real, imag) for mode in range(MODES)]
        waves = [turned(wave) for wave in run(waves, forward)]
        waves = [times_conj(wave, turn[0], turn[1]) for wave in run(waves, forward)]
        waves = [turned(wave) for wave in run(waves, inverse)]
        waves = run(waves, inverse)
        for mode in range(MODES):
            current[mode] = waves[mode]

    def deliver(index, lags):
        for lag, action in lags:
            late = index + lag

            @pl.when((late >= 0) & (late < SLICES) & (late // LOCAL == section))
            def _():
                action(late)

    late_lags = ((LAG_GATHER, sort_groups), (LAG_TERMS, gather_terms), (LAG_RIM, finish))
    lags = ((LAG_TERMS, gather_terms), (LAG_GATHER, sort_groups), (LAG_RIM, finish))

    def backward_step(step, carry):
        index = SLICES - 1 - step
        hand_over(index)
        retreat(index)
        collect(index - 1)
        deliver(index, lags)
        return carry

    collect(SLICES - 1)
    lax.fori_loop(0, SLICES - 1, backward_step, 0)
    hand_over(0)

    def drain_step(step, carry):
        deliver(-step, late_lags)
        return carry

    lax.fori_loop(0, LAG_RIM + 1, drain_step, 0)

    for distance in (1, 3, 2):
        for local in range(LOCAL):
            out_copy(local, distance, behind(distance)).wait_recv()

    def drain(local, carry):
        halo_copy(local).wait_send()
        window_copy(section * LOCAL + local).wait_send()
        terms_copy((1 - section) * LOCAL + local).wait_send()
        rim_copy(local).wait_send()
        for distance in (1, 2, 3):
            group_copy(local, distance).wait_send()
            out_copy(local, distance, me).wait_send()
        return carry

    lax.fori_loop(0, LOCAL, drain, 0)


def body(object_slices, probe_modes, propagator_phase, measured, row_offset, col_offset, counts):
    square = (W, W)
    vmem = lambda *shape: pltpu.VMEM(shape, jnp.float32)
    dma = lambda *shape: pltpu.SemaphoreType.DMA(shape)
    smem_spec = pl.BlockSpec(memory_space=pltpu.SMEM)
    vmem_spec = pl.BlockSpec(memory_space=pltpu.VMEM)
    hbm_spec = pl.BlockSpec(memory_space=pltpu.HBM)
    operands = (
        row_offset, col_offset, counts, probe_modes, object_slices, propagator_phase, measured,
        jnp.asarray(tables()),
    )
    operands = [
        operand if operand is counts else pltpu.with_memory_space_constraint(operand, pltpu.HBM)
        for operand in operands
    ]
    return pl.pallas_call(
        kernel,
        out_shape=jax.ShapeDtypeStruct((2, LOCAL) + square, jnp.float32),
        in_specs=[hbm_spec] * 2 + [smem_spec] + [hbm_spec] * 5,
        out_specs=vmem_spec,
        scratch_shapes=[
            pltpu.SMEM((SLOTS,), jnp.int32), pltpu.SMEM((SLOTS,), jnp.int32),
            vmem(*object_slices.shape), vmem(*square), vmem(*square),
            pltpu.VMEM((4, 2 * W, 2 * W), jnp.bfloat16),
            pltpu.VMEM((INFO, W), jnp.int32), pltpu.VMEM((INFO, W), jnp.int32),
            pltpu.SMEM((INFO, W), jnp.int32),
            pltpu.VMEM((SLOTS, ROW_GROUP, W), jnp.int32),
            vmem(MODES, 2, *square),
            vmem(LOCAL, 2, *square), vmem(LOCAL, 2, *square),
            vmem(SLICES, 2, *square),
            vmem(SLICES, MODES, W, 2 * W),
            vmem(2, *square),
            vmem(MODES, W, 2 * W), vmem(MODES, W, 2 * W),
            vmem(*square), vmem(*square),
            vmem(SLICES, 2, *square), vmem(LOCAL, 2, *square),
            vmem(LOCAL, 2, *square),
            vmem(LOCAL, SLOTS, 2, ROW_GROUP, W),
            vmem(LOCAL, SLOTS, 2, ROW_GROUP, W), vmem(LOCAL, SLOTS, 2, ROW_GROUP, W),
            vmem(LOCAL, SLOTS, 2, ROW_GROUP, W),
            dma(2), dma(5), dma(2), dma(2), dma(4), dma(4), dma(LOCAL), dma(LOCAL),
            dma(SLICES), dma(SLICES), dma(2), dma(LOCAL), dma(LOCAL),
            dma(LOCAL, SLOTS), dma(LOCAL, SLOTS), dma(LOCAL), dma(LOCAL),
            dma(LOCAL, SLOTS), dma(LOCAL, SLOTS),
        ],
        compiler_params=pltpu.CompilerParams(
            collective_id=0, has_side_effects=True, vmem_limit_bytes=40 * 1024 * 1024
        ),
    )(*operands)


def solution(mesh):
    in_specs = (
        P(None, "section", "tile", None),
        P(None, "mode", None, None),
        P(),
        P("tile", None, None),
        P("tile"),
        P("tile"),
        P("tile"),
    )
    out_specs = P(None, "section", "tile", "mode")
    return jax.shard_map(body, mesh=mesh, in_specs=in_specs, out_specs=out_specs, check_vma=False)
```
